32 devices in a mesh: dp: 4 (over y, core), expert: 8 (over z, x).
Axes of the slice: x: 2, y: 2, z: 4, core: 2. Of those that a mesh axis runs over, the one named last changes fastest.
Arguments:
- frames: bfloat16 [4096, 1024], P(('dp', 'expert')), may hold values from -6 to 6
- cotangent: bfloat16 [4096, 1024], P(('dp', 'expert')), may hold values from -6 to 6
- expert_ids: int32 [4096, 1], P(('dp', 'expert')), may hold values from 0 to 7; in each aligned block of 128 rows (0 to 127, 128 to 255, ...) at most 32 rows name the same one
- conv_weight: float32 [32, 1024], replicated, may hold values from -1 to 1
- up_master: float32 [8, 1024, 2048], P('expert', 'dp'), may hold values from -0.1875 to 0.1875
- down_master: float32 [8, 2048, 1024], P('expert', 'dp'), may hold values from -0.125 to 0.125
- up_mean_code: bfloat16 [8, 1024, 2048], P('expert', 'dp'), may hold values from -1 to 1
- up_mean_scale: float32 [8, 1024, 16], P('expert', 'dp'), may hold values from 0.5 to 5
- up_square_code: bfloat16 [8, 1024, 2048], P('expert', 'dp'), may hold values from 0.049804688 to 1
- up_square_scale: float32 [8, 1024, 16], P('expert', 'dp'), may hold values from 20 to 200
- down_mean_code: bfloat16 [8, 2048, 1024], P('expert', 'dp'), may hold values from -1 to 1
- down_mean_scale: float32 [8, 2048, 8], P('expert', 'dp'), may hold values from 0.5 to 5
- down_square_code: bfloat16 [8, 2048, 1024], P('expert', 'dp'), may hold values from 0.049804688 to 1
- down_square_scale: float32 [8, 2048, 8], P('expert', 'dp'), may hold values from 20 to 200
Outputs:
- grad_frames: bfloat16 [4096, 1024], P(('dp', 'expert'))
- conv_grad: float32 [32, 1024], replicated
- up_next: float32 [8, 1024, 2048], P('expert', 'dp')
- up_mean_next: bfloat16 [8, 1024, 2048], P('expert', 'dp')
- up_mean_scale_next: float32 [8, 1024, 16], P('expert', 'dp')
- up_square_next: bfloat16 [8, 1024, 2048], P('expert', 'dp')
- up_square_scale_next: float32 [8, 1024, 16], P('expert', 'dp')
- down_next: float32 [8, 2048, 1024], P('expert', 'dp')
- down_mean_next: bfloat16 [8, 2048, 1024], P('expert', 'dp')
- down_mean_scale_next: float32 [8, 2048, 8], P('expert', 'dp')
- down_square_next: bfloat16 [8, 2048, 1024], P('expert', 'dp')
- down_square_scale_next: float32 [8, 2048, 8], P('expert', 'dp')
The draws below stay inside these ranges and needn't reach their ends.
Inputs may be any that keep to these rules, and one draw needn't show every extreme that they name: `expert_ids`: within each device's aligned block of 128 frames no expert is chosen by more than 32 frames, and some expert is chosen by exactly 32 frames.
All inputs are finite; a program needn't handle non-finite values. Where the reference program divides by a largest or mean magnitude, that divisor is 1e-20 or more.
Results may differ from the reference program's by a relative error of at most 0.017.
Values may be sent and summed in bfloat16 or wider, within the bound.
No kernel may reach another device: no remote copies, remote signals or barrier semaphores. Data moves between devices by JAX's collectives and lax.ppermute only.
A program may use at most 128 MiB of HBM per device.

```python
import math
import jax
import jax.numpy as jnp
import numpy as np
from jax import lax

D = 1024
H = 2048
K = 32
QB = 128
F_DEV = 128
EXPERTS = 8
GROUPS = 4
CAP = 32
GROUP_FRAMES = 1024
FRAMES = 4096


def levels(rng, dims, split, low, top_value):
    gain = 1.0
    for position, blocks in split:
        heights = jax.random.uniform(jax.random.fold_in(jax.random.fold_in(rng, 6), position), (blocks,), jnp.float32, low / len(split), top_value / len(split))
        gain = gain * jnp.repeat(jnp.exp(heights), dims[position] // blocks).reshape((-1,) + (1,) * (len(dims) - 1 - position))
    return gain


def shared_out(rng, own, number, rows, amount, top, most, slope):
    order = jax.random.permutation(rng, amount)
    packed, usual = load_shares(amount, rows * top, most, slope, True), load_shares(amount, rows * top, most, slope, False)
    places = jnp.arange(amount)

    def named(tallies, rotation):
        used = int((tallies > 0).sum())
        fixed = max(1, used // 4)
        shifted = fixed + (places - fixed + rotation * (used - fixed)) % max(1, amount - fixed)
        return jnp.zeros((amount,), jnp.int32).at[order[jnp.where(places < fixed, places, shifted)]].set(jnp.asarray(tallies, jnp.int32))

    tallies = jnp.where(number % 4 == 0, named(packed, number // 4), named(usual, number - number // 4 - 1))
    mixed = jax.random.permutation(jax.random.fold_in(own, 3), amount)
    source_of, sink = mixed[0:amount // 2 * 2:2], mixed[1:amount // 2 * 2:2]
    slack = jnp.minimum(tallies[source_of] - 1, most - tallies[sink]) // 2
    slack = jnp.where((source_of == order[0]) | (sink == order[0]) | (tallies[sink] == 0), 0, jnp.maximum(slack, 0))
    shifted = jax.random.randint(jax.random.fold_in(own, 4), (amount // 2,), 0, 1 << 20) % (slack + 1)
    tallies = tallies.at[source_of].add(-shifted).at[sink].add(shifted)
    labels = jnp.searchsorted(jnp.cumsum(tallies), jnp.arange(rows * top), side="right").astype(jnp.int32)
    grid = labels.reshape(top, rows).T
    grid = grid[jax.random.permutation(jax.random.fold_in(own, 1), rows)]
    rotation = jax.random.randint(jax.random.fold_in(own, 2), (rows, 1), 0, top)
    return jnp.take_along_axis(grid, (jnp.arange(top)[None, :] + rotation) % top, axis=1)


def load_shares(count, total, limit, slope, full):
    weights = [(1 << 20) // math.isqrt(standing ** slope) + 1 for standing in range(1, count + 1)]
    largest = limit if full else min(limit, max(-(-total // count), total * weights[0] // sum(weights)))
    least = 1 if total - largest >= count - 1 else 0
    counts, rest = [largest] + [least] * (count - 1), total - largest - least * (count - 1)
    while rest > 0:
        movable = [i for i in range(1, count) if counts[i] < largest] or [i for i in range(1, count) if counts[i] < limit]
        whole, budget = sum([weights[i] for i in movable]), rest
        for i in movable:
            addition = min(limit - counts[i], max(1, budget * weights[i] // whole), rest)
            counts[i] = counts[i] + addition
            rest = rest - addition
    return np.array(counts)


def noise(stream_key, shape, width, most, pieces=(), kind=jnp.bfloat16):
    entries = width * jax.random.normal(stream_key, shape, jnp.float32)
    if pieces:
        entries = entries * levels(stream_key, shape, pieces, -0.22, 0.18)
    return jnp.clip(entries, -most, most).astype(kind)


def setup_inputs(seed: int = 0) -> dict:
    seeds = jax.random.split(jax.random.key(seed), 15)
    frames = noise(seeds[0], (FRAMES, D), 1.0, 6.0, ((0, 32),))
    cotangent = noise(seeds[1], (FRAMES, D), 1.0, 6.0, ((0, 32),))
    expert_ids_keys = jax.random.split(jax.random.fold_in(seeds[2], 1), FRAMES // F_DEV)
    expert_ids_turns = jax.random.permutation(jax.random.fold_in(seeds[2], 3), FRAMES // F_DEV)
    expert_ids = jax.vmap(lambda own, number: shared_out(jax.random.fold_in(seeds[2], 2), own, number, F_DEV, EXPERTS, 1, CAP, 1))(expert_ids_keys, expert_ids_turns).reshape((FRAMES, 1))
    conv_weight = noise(seeds[3], (K, D), K ** -0.5, 1.0, (), jnp.float32)
    up_master = noise(seeds[4], (EXPERTS, D, H), D ** -0.5, 0.1875, ((0, 8), (1, 4)), jnp.float32)
    down_master = noise(seeds[5], (EXPERTS, H, D), H ** -0.5, 0.125, ((0, 8), (1, 4)), jnp.float32)
    up_mean_code = jnp.clip(jax.random.uniform(seeds[6], (EXPERTS, D, H), jnp.float32, -1.0, 1.0) * levels(seeds[6], (EXPERTS, D, H), ((0, 8), (1, 4)), -0.4, 0.0), -1.0, 1.0).astype(jnp.bfloat16)
    up_mean_scale = jnp.clip(jnp.exp(math.log(5.0) - 2.3025851 * jax.random.uniform(seeds[7], (EXPERTS, D, H // QB), jnp.float32) ** levels(seeds[7], (EXPERTS, D, H // QB), ((0, 8), (1, 4)), -0.2, 0.2)), 0.5, 5.0)
    up_square_code = jnp.clip(0.049804688 + 0.9501953 * jax.random.uniform(seeds[8], (EXPERTS, D, H), jnp.float32) ** levels(seeds[8], (EXPERTS, D, H), ((0, 8), (1, 4)), -0.2, 0.2), 0.049804688, 1.0).astype(jnp.bfloat16)
    up_square_scale = jnp.clip(jnp.exp(math.log(200.0) - 2.3025851 * jax.random.uniform(seeds[9], (EXPERTS, D, H // QB), jnp.float32) ** levels(seeds[9], (EXPERTS, D, H // QB), ((0, 8), (1, 4)), -0.2, 0.2)), 20.0, 200.0)
    down_mean_code = jnp.clip(jax.random.uniform(seeds[10], (EXPERTS, H, D), jnp.float32, -1.0, 1.0) * levels(seeds[10], (EXPERTS, H, D), ((0, 8), (1, 4)), -0.4, 0.0), -1.0, 1.0).astype(jnp.bfloat16)
    down_mean_scale = jnp.clip(jnp.exp(math.log(5.0) - 2.3025851 * jax.random.uniform(seeds[11], (EXPERTS, H, D // QB), jnp.float32) ** levels(seeds[11], (EXPERTS, H, D // QB), ((0, 8), (1, 4)), -0.2, 0.2)), 0.5, 5.0)
    down_square_code = jnp.clip(0.049804688 + 0.9501953 * jax.random.uniform(seeds[12], (EXPERTS, H, D), jnp.float32) ** levels(seeds[12], (EXPERTS, H, D), ((0, 8), (1, 4)), -0.2, 0.2), 0.049804688, 1.0).astype(jnp.bfloat16)
    down_square_scale = jnp.clip(jnp.exp(math.log(200.0) - 2.3025851 * jax.random.uniform(seeds[13], (EXPERTS, H, D // QB), jnp.float32) ** levels(seeds[13], (EXPERTS, H, D // QB), ((0, 8), (1, 4)), -0.2, 0.2)), 20.0, 200.0)
    return dict(frames=frames, cotangent=cotangent, expert_ids=expert_ids, conv_weight=conv_weight, up_master=up_master, down_master=down_master, up_mean_code=up_mean_code, up_mean_scale=up_mean_scale, up_square_code=up_square_code, up_square_scale=up_square_scale, down_mean_code=down_mean_code, down_mean_scale=down_mean_scale, down_square_code=down_square_code, down_square_scale=down_square_scale)


beta_one = 0.9
beta_two = 0.95
bias_one = 1.0 - beta_one ** 10
bias_two = 1.0 - beta_two ** 10
learn_rate = 0.001
adam_eps = 1e-08
scale_eps = 1e-06

def swish_parts(values):
    gate_value = jax.nn.sigmoid(values)
    return (values * gate_value, gate_value * (1.0 + values * (1.0 - gate_value)))

def round_trip(values):
    return lax.optimization_barrier(values.astype(jnp.bfloat16)).astype(jnp.float32)

def adam_block(master, gradient, mean_code, mean_scale, square_code, square_scale):
    full_shape = master.shape
    block_count = mean_scale.shape[-1]
    blocked = full_shape[:-1] + (block_count, full_shape[-1] // block_count)
    mean_old = mean_code.astype(jnp.float32).reshape(blocked) * mean_scale[..., None]
    square_old = square_code.astype(jnp.float32).reshape(blocked) * square_scale[..., None]
    grad_blocks = gradient.reshape(blocked)
    mean_new = beta_one * mean_old + (1.0 - beta_one) * grad_blocks
    square_new = beta_two * square_old + (1.0 - beta_two) * grad_blocks * grad_blocks
    update = mean_new / bias_one / (jnp.sqrt(square_new / bias_two) + adam_eps)
    master_new = master - learn_rate * update.reshape(full_shape)
    mean_top = lax.optimization_barrier(jnp.max(jnp.abs(mean_new), axis=-1)) + scale_eps
    square_top = lax.optimization_barrier(jnp.max(square_new, axis=-1)) + scale_eps
    mean_codes = (mean_new / mean_top[..., None]).reshape(full_shape).astype(jnp.bfloat16)
    square_codes = (square_new / square_top[..., None]).reshape(full_shape).astype(jnp.bfloat16)
    return (master_new, mean_codes, mean_top, square_codes, square_top)

def reference(frames, cotangent, expert_ids, conv_weight, up_master, down_master, up_mean_code, up_mean_scale, up_square_code, up_square_scale, down_mean_code, down_mean_scale, down_square_code, down_square_scale):
    half_taps = K // 2
    frames_f = frames.astype(jnp.float32)
    padded = jnp.pad(frames_f, ((half_taps, half_taps), (0, 0)))
    convolved = jnp.zeros((FRAMES, D), jnp.float32)
    for tap_index in range(K):
        convolved = convolved + conv_weight[tap_index] * padded[tap_index:tap_index + FRAMES]
    activated, conv_slope = swish_parts(convolved)
    features = activated.astype(jnp.bfloat16)
    chosen = expert_ids[:, 0].astype(jnp.int32)
    blocks = chosen.reshape(-1, F_DEV)
    one_hot = (blocks[:, :, None] == jnp.arange(EXPERTS, dtype=jnp.int32)[None, None, :]).astype(jnp.int32)
    ranks = jnp.cumsum(one_hot, axis=1) - one_hot
    slot_index = lax.optimization_barrier(jnp.sum(ranks * one_hot, axis=2)).reshape(-1)
    source = jnp.arange(FRAMES, dtype=jnp.int32) // F_DEV % EXPERTS
    flat_index = chosen * (EXPERTS * CAP) + source * CAP + slot_index
    up_weight = up_master.astype(jnp.bfloat16).astype(jnp.float32)
    down_weight = down_master.astype(jnp.bfloat16).astype(jnp.float32)
    up_grad = jnp.zeros((EXPERTS, D, H), jnp.float32)
    down_grad = jnp.zeros((EXPERTS, H, D), jnp.float32)
    grad_pieces = []
    for group_index in range(GROUPS):
        lower = group_index * GROUP_FRAMES
        group_flat = flat_index[lower:lower + GROUP_FRAMES]
        empty_rows = jnp.zeros((EXPERTS * EXPERTS * CAP, D), jnp.float32)
        rows_in = empty_rows.at[group_flat].set(features[lower:lower + GROUP_FRAMES].astype(jnp.float32)).reshape(EXPERTS, EXPERTS * CAP, D)
        grads_in = empty_rows.at[group_flat].set(cotangent[lower:lower + GROUP_FRAMES].astype(jnp.float32)).reshape(EXPERTS, EXPERTS * CAP, D)
        pre_act = jnp.einsum('erd,edh->erh', rows_in, up_weight)
        hidden_act, hidden_slope = swish_parts(pre_act)
        hidden = round_trip(hidden_act)
        down_part = jnp.einsum('erh,erd->ehd', hidden, grads_in)
        grad_hidden = jnp.einsum('erd,ehd->erh', grads_in, down_weight)
        grad_pre = round_trip(grad_hidden * hidden_slope)
        up_part = jnp.einsum('erd,erh->edh', rows_in, grad_pre)
        grad_rows = jnp.einsum('erh,edh->erd', grad_pre, up_weight).astype(jnp.bfloat16)
        grad_pieces.append(grad_rows.reshape(-1, D)[group_flat])
        up_grad = up_grad + round_trip(up_part)
        down_grad = down_grad + round_trip(down_part)
    grad_features = jnp.concatenate(grad_pieces, axis=0)
    grad_conv = (grad_features.astype(jnp.float32) * conv_slope).astype(jnp.bfloat16)
    grad_conv_f = grad_conv.astype(jnp.float32)
    grad_padded = jnp.pad(grad_conv_f, ((half_taps, half_taps), (0, 0)))
    grad_total = cotangent.astype(jnp.float32)
    for tap_index in range(K):
        grad_total = grad_total + conv_weight[tap_index] * grad_padded[K - tap_index:K - tap_index + FRAMES]
    grad_frames = grad_total.astype(jnp.bfloat16)
    conv_grad = jnp.stack([lax.optimization_barrier(jnp.sum(grad_conv_f * padded[tap_index:tap_index + FRAMES], axis=0)) for tap_index in range(K)])
    up_next, up_mean_next, up_mean_scale_next, up_square_next, up_square_scale_next = adam_block(up_master, up_grad, up_mean_code, up_mean_scale, up_square_code, up_square_scale)
    down_next, down_mean_next, down_mean_scale_next, down_square_next, down_square_scale_next = adam_block(down_master, down_grad, down_mean_code, down_mean_scale, down_square_code, down_square_scale)
    return (grad_frames, conv_grad, up_next, up_mean_next, up_mean_scale_next, up_square_next, up_square_scale_next, down_next, down_mean_next, down_mean_scale_next, down_square_next, down_square_scale_next)
```

```python
import functools

import jax
import jax.numpy as jnp
from jax import lax
from jax.experimental import pallas as pl
from jax.experimental.pallas import tpu as pltpu
from jax.sharding import PartitionSpec as P

beta_one = 0.9
beta_two = 0.95
bias_one = 1.0 - beta_one**10
bias_two = 1.0 - beta_two**10
learn_rate = 0.001
adam_eps = 1e-08
scale_eps = 1e-06

f32 = jnp.float32
bf16 = jnp.bfloat16
MIB = 1 << 20


def swish_parts(values):
    gate_value = 1.0 / (1.0 + jnp.exp(-values))
    return (values * gate_value, gate_value * (1.0 + values * (1.0 - gate_value)))


def across(lhs, rhs):
    return lax.dot_general(lhs, rhs, (((0,), (0,)), ((), ())), preferred_element_type=f32)


def along(lhs, rhs):
    return lax.dot_general(lhs, rhs, (((1,), (1,)), ((), ())), preferred_element_type=f32)


def staged(kernel, counts, spans, *refs):
    groups = []
    for count in counts:
        groups.append(refs[:count])
        refs = refs[count:]
    scalars, sources, targets, held, made, scratch = groups
    in_sems, out_sems = refs
    arriving = []
    for index, source in enumerate(sources):
        if spans[index] is not None:
            source = source.at[pl.ds(*spans[index]), :]
        copy = pltpu.make_async_copy(source, held[index], in_sems.at[index])
        copy.start()
        arriving.append(copy)
    leaving = {}

    def take(index):
        if arriving[index] is not None:
            arriving[index].wait()
            arriving[index] = None
        return held[index]

    def give(index):
        leaving[index] = pltpu.make_async_copy(made[index], targets[index], out_sems.at[index])
        leaving[index].start()

    kernel(scalars, take, made, give, scratch)
    for index in range(len(targets)):
        if index not in leaving:
            give(index)
    for index in range(len(sources)):
        take(index)
    for copy in leaving.values():
        copy.wait()


def call(kernel, name, scalars, inputs, outs, scratch=(), flops=0, moved=0, limit=40):
    hbm = pl.BlockSpec(memory_space=pltpu.HBM)
    smem = pl.BlockSpec(memory_space=pltpu.SMEM)
    pairs = [item if isinstance(item, tuple) else (item, None) for item in inputs]
    arrays = [array for array, _ in pairs]
    spans = [span for _, span in pairs]
    held = [
        pltpu.VMEM(array.shape if span is None else (span[1],) + array.shape[1:], array.dtype)
        for array, span in pairs
    ]
    made = [pltpu.VMEM(shape, kind) for shape, kind in outs]
    counts = (len(scalars), len(arrays), len(outs), len(held), len(made), len(scratch))
    return pl.pallas_call(
        functools.partial(staged, kernel, counts, spans),
        out_shape=[jax.ShapeDtypeStruct(shape, kind) for shape, kind in outs],
        in_specs=[smem] * len(scalars) + [hbm] * len(arrays),
        out_specs=[hbm] * len(outs),
        scratch_shapes=held
        + made
        + list(scratch)
        + [pltpu.SemaphoreType.DMA((len(arrays),)), pltpu.SemaphoreType.DMA((len(outs),))],
        compiler_params=pltpu.CompilerParams(vmem_limit_bytes=limit * MIB),
        cost_estimate=pl.CostEstimate(flops=flops, bytes_accessed=moved, transcendentals=0),
        name=name,
    )(*scalars, *arrays)


def dispatch_kernel(experts, capacity, scalars, take, made, give, scratch):
    place_ref, out_ref = made
    ids = take(0)[...]
    length = ids.shape[1]
    rows = lax.broadcasted_iota(jnp.int32, (experts, length), 0)
    one_hot = (rows == ids).astype(f32)
    earlier = lax.broadcasted_iota(jnp.int32, (length, length), 0)
    later = lax.broadcasted_iota(jnp.int32, (length, length), 1)
    ranks = jnp.dot(one_hot, (earlier < later).astype(f32), preferred_element_type=f32)
    slot = jnp.sum(ranks * one_hot, axis=0, keepdims=True).astype(jnp.int32)
    position = ids * capacity + slot
    slots = lax.broadcasted_iota(jnp.int32, (experts * capacity, length), 0)
    place = (slots == position).astype(f32).astype(bf16)
    place_ref[...] = place
    out_ref[...] = jnp.dot(place, take(1)[...], preferred_element_type=f32).astype(bf16)


def fill_padded(pad_ref, left_ref, middle_ref, right_ref):
    side, length = left_ref.shape[0], middle_ref.shape[0]
    pad_ref[0:side, :] = left_ref[...].astype(f32)
    pad_ref[side : side + length, :] = middle_ref[...].astype(f32)
    pad_ref[side + length : side + length + side, :] = right_ref[...].astype(f32)


def conv_kernel(scalars, take, made, give, scratch):
    slope_ref, out_ref = made
    pad_ref, feat_ref = scratch
    fill_padded(pad_ref, take(0), take(1), take(2))
    taps_ref = take(3)
    length, width = feat_ref.shape

    def lanes(step, carry):
        cols = pl.ds(pl.multiple_of(step * 128, 128), 128)
        total = jnp.zeros((length, 128), f32)
        for tap in range(taps_ref.shape[0]):
            total = total + taps_ref[tap : tap + 1, cols] * pad_ref[tap : tap + length, cols]
        active, slope = swish_parts(total)
        slope_ref[:, cols] = slope
        feat_ref[:, cols] = active.astype(bf16)
        return carry

    lax.fori_loop(0, width // 128, lanes, 0)
    out_ref[...] = jnp.dot(take(4)[...], feat_ref[...], preferred_element_type=f32).astype(bf16)


def forward_kernel(shards, scalars, take, made, give, scratch):
    (order_ref,) = scalars
    slope_ref, keep_ref, send_ref = made
    (hidden_ref,) = scratch
    rows_ref = take(0)
    up_refs = [take(2 + shard) for shard in range(shards)]
    slots, width = rows_ref.shape
    depth = width // shards
    chunk = 512

    for half in range(hidden_ref.shape[1] // width):

        def step(index, carry):
            start = pl.multiple_of(index * chunk, chunk)
            cols = pl.ds(start, chunk)
            pre = 0.0
            for shard, up_ref in enumerate(up_refs):
                at = pl.ds(pl.multiple_of(order_ref[shard] * depth, depth), depth)
                weight = up_ref[half * depth : (half + 1) * depth, cols]
                pre = pre + jnp.dot(rows_ref[:, at], weight, preferred_element_type=f32)
            active, slope = swish_parts(pre)
            spot = pl.ds(pl.multiple_of(half * width + start, chunk), chunk)
            hidden_ref[:, spot] = active.astype(bf16)
            slope_ref[:, spot] = slope
            return carry

        lax.fori_loop(0, width // chunk, step, 0)
    give(0)
    grads = take(1)[...]
    share = hidden_ref.shape[1] // shards
    for out_ref, side in ((send_ref, 1), (keep_ref, 0)):
        for index in range(shards // 2):
            place = order_ref[shards + 2 * index + side]
            at = pl.ds(pl.multiple_of(place * share, share), share)
            out_ref[index * share : (index + 1) * share, :] = across(
                hidden_ref[:, at], grads
            ).astype(bf16)
        give(1 if out_ref is keep_ref else 2)


def backward_kernel(shards, scalars, take, made, give, scratch):
    (order_ref,) = scalars
    pre_ref, out_ref = made
    grads_ref = take(0)
    slope_ref = take(1)
    slots, width = grads_ref.shape
    hidden = pre_ref.shape[1]
    share, depth = hidden // shards, width // shards
    for shard in range(shards):
        at = pl.ds(pl.multiple_of(order_ref[shard] * share, share), share)
        back = along(grads_ref[...], take(2 + shard)[...])
        pre_ref[:, at] = (back * slope_ref[:, at]).astype(bf16)
    give(0)
    for shard in range(shards):
        at = pl.ds(pl.multiple_of(order_ref[shard] * depth, depth), depth)
        up_ref = take(2 + shards + shard)
        back = 0.0
        for half in range(hidden // width):
            back = back + along(
                pre_ref[:, half * width : (half + 1) * width],
                up_ref[half * depth : (half + 1) * depth, :],
            )
        out_ref[:, at] = back.astype(bf16)


def up_grad_kernel(shards, scalars, take, made, give, scratch):
    (order_ref,) = scalars
    keep_ref, send_ref = made
    rows_ref, pre = take(0), take(1)[...]
    depth = rows_ref.shape[1] // shards
    for out_ref, side in ((send_ref, 1), (keep_ref, 0)):
        for index in range(shards // 2):
            place = order_ref[shards + 2 * index + side]
            at = pl.ds(pl.multiple_of(place * depth, depth), depth)
            out_ref[index * depth : (index + 1) * depth, :] = across(
                rows_ref[:, at], pre
            ).astype(bf16)
        give(0 if out_ref is keep_ref else 1)


def cast_kernel(scalars, take, made, give, scratch):
    up_ref, down_ref, both_ref = made
    up, down = take(0), take(1)
    depth, hidden = up.shape
    share, width = down.shape
    for half in range(hidden // width):
        values = up[:, half * width : (half + 1) * width].astype(bf16)
        up_ref[half * depth : (half + 1) * depth, :] = values
        both_ref[half * depth : (half + 1) * depth, :] = values
    give(0)
    values = down[...].astype(bf16)
    down_ref[...] = values
    both_ref[share : 2 * share, :] = values


def taps_kernel(scalars, take, made, give, scratch):
    grad_ref, head_ref, tail_ref, terms_ref = made
    (pad_ref,) = scratch
    fill_padded(pad_ref, take(2), take(3), take(4))
    length, width = grad_ref.shape
    side = head_ref.shape[0]
    features = across(take(0)[...], take(5)[...]).astype(bf16).astype(f32)
    grad = (features * take(1)[...]).astype(bf16)
    grad_ref[...] = grad
    head_ref[...] = grad[:side]
    tail_ref[...] = grad[length - side :]
    give(1)
    give(2)
    give(0)

    def lanes(step, carry):
        cols = pl.ds(pl.multiple_of(step * 128, 128), 128)
        local = grad_ref[:, cols].astype(f32)
        for tap in range(terms_ref.shape[0]):
            product = local * pad_ref[tap : tap + length, cols]
            terms_ref[tap : tap + 1, cols] = jnp.sum(product, axis=0, keepdims=True)
        return carry

    lax.fori_loop(0, width // 128, lanes, 0)


def frames_kernel(scalars, take, made, give, scratch):
    (out_ref,) = made
    (pad_ref,) = scratch
    length, width = out_ref.shape
    fill_padded(pad_ref, take(0), take(1), take(2))
    taps_ref, cot_ref = take(3), take(4)
    count = taps_ref.shape[0]

    def lanes(step, carry):
        cols = pl.ds(pl.multiple_of(step * 128, 128), 128)
        total = cot_ref[:, cols].astype(f32)
        for tap in range(count):
            start = count - tap
            total = total + taps_ref[tap : tap + 1, cols] * pad_ref[start : start + length, cols]
        out_ref[:, cols] = total.astype(bf16)
        return carry

    lax.fori_loop(0, width // 128, lanes, 0)


def adam_kernel(terms, master_ref, mean_ref, mean_scale_ref, square_ref, square_scale_ref, *refs):
    grad_refs, refs = refs[:terms], refs[terms:]
    next_ref, mean_next_ref, mean_top_ref, square_next_ref, square_top_ref = refs[:5]
    scales_ref, tops_ref = refs[5:]
    rows, width = master_ref.shape
    blocks = mean_scale_ref.shape[0]
    size = width // blocks
    step = pl.program_id(0)
    steps = pl.num_programs(0)

    @pl.when(step == 0)
    def _():
        scales_ref[0, :, :blocks] = mean_scale_ref[...].T
        scales_ref[1, :, :blocks] = square_scale_ref[...].T

    here = pl.ds(pl.multiple_of(step * rows, rows), rows)
    mean_scales = scales_ref[0, here, :]
    square_scales = scales_ref[1, here, :]
    for block in range(blocks):
        cols = slice(block * size, (block + 1) * size)
        grad = grad_refs[0][:, cols].astype(f32)
        for grad_ref in grad_refs[1:]:
            grad = grad + grad_ref[:, cols].astype(f32)
        mean = beta_one * (
            mean_ref[:, cols].astype(f32) * mean_scales[:, block : block + 1]
        ) + (1.0 - beta_one) * grad
        square = beta_two * (
            square_ref[:, cols].astype(f32) * square_scales[:, block : block + 1]
        ) + (1.0 - beta_two) * (grad * grad)
        root = jnp.sqrt(square * (1.0 / bias_two)) + adam_eps
        next_ref[:, cols] = master_ref[:, cols] - (learn_rate / bias_one) * (mean / root)
        mean_top = jnp.max(jnp.abs(mean), axis=1, keepdims=True) + scale_eps
        square_top = jnp.max(square, axis=1, keepdims=True) + scale_eps
        mean_next_ref[:, cols] = (mean * (1.0 / mean_top)).astype(bf16)
        square_next_ref[:, cols] = (square * (1.0 / square_top)).astype(bf16)
        tops_ref[0, here, block : block + 1] = mean_top
        tops_ref[1, here, block : block + 1] = square_top

    @pl.when(step == steps - 1)
    def _():
        mean_top_ref[...] = tops_ref[0, :, :blocks].T
        square_top_ref[...] = tops_ref[1, :, :blocks].T


def adam(name, master, grads, mean_code, mean_scale, square_code, square_scale):
    _, rows, width = master.shape
    blocks = mean_scale.shape[-1]
    part = 32
    tile = pl.BlockSpec((part, width), lambda i: (i, 0))
    whole = pl.BlockSpec((blocks, rows), lambda i: (0, 0))
    wide = jax.ShapeDtypeStruct((rows, width), f32)
    code = jax.ShapeDtypeStruct((rows, width), bf16)
    scale = jax.ShapeDtypeStruct((blocks, rows), f32)
    results = pl.pallas_call(
        functools.partial(adam_kernel, len(grads)),
        grid=(rows // part,),
        out_shape=[wide, code, scale, code, scale],
        in_specs=[tile, tile, whole, tile, whole] + [tile] * len(grads),
        out_specs=[tile, tile, whole, tile, whole],
        scratch_shapes=[pltpu.VMEM((2, rows, 128), f32), pltpu.VMEM((2, rows, 128), f32)],
        compiler_params=pltpu.CompilerParams(vmem_limit_bytes=32 * MIB),
        cost_estimate=pl.CostEstimate(
            flops=20 * rows * width,
            bytes_accessed=(16 + 2 * len(grads)) * rows * width,
            transcendentals=0,
        ),
        name=name,
    )(master[0], mean_code[0], mean_scale[0].T, square_code[0], square_scale[0].T, *grads)
    new_master, mean_next, mean_top, square_next, square_top = results
    return (new_master[None], mean_next[None], mean_top.T[None], square_next[None], square_top.T[None])


def by_expert(rows):
    experts = lax.axis_size("expert")
    slots, width = rows.shape
    cells = rows.reshape(experts, slots // experts, width)
    return lax.all_to_all(cells, "expert", 0, 0, tiled=True).reshape(slots, width)


def to_chip(values, shift):
    count = lax.axis_size("dp")
    chips = count // 2
    return lax.ppermute(
        values, "dp", [(i, (i // 2 + shift) % chips * 2 + i % 2) for i in range(count)]
    )


def to_core(values):
    count = lax.axis_size("dp")
    return lax.ppermute(values, "dp", [(i, i ^ 1) for i in range(count)])


def gather_shards(up_shard, down_shard, both):
    chips = lax.axis_size("dp") // 2
    share = up_shard.shape[0]
    upper, lower = (0, share), (share, share)
    near = to_core(both)
    ups, downs = [(both, upper), (near, upper)], [(both, lower), (near, lower)]
    far_ups = [to_chip(up_shard, shift) for shift in range(1, chips)]
    far_downs = [to_chip(down_shard, shift) for shift in range(1, chips)]
    for arrived in far_ups:
        ups = ups + [arrived, to_core(arrived)]
    for arrived in far_downs:
        downs = downs + [arrived, to_core(arrived)]
    return ups, downs


def sum_shares(keep, send):
    chips = lax.axis_size("dp") // 2
    theirs = to_core(send)
    share = keep.shape[0] // chips
    grads = [keep, theirs]
    for shift in range(1, chips):
        part = slice(shift * share, (shift + 1) * share)
        chip_sum = (keep[part].astype(f32) + theirs[part].astype(f32)).astype(bf16)
        grads.append(to_chip(chip_sum, shift))
    return grads


def halo(head, tail):
    axes = ("dp", "expert")
    count = lax.axis_size("dp") * lax.axis_size("expert")
    right = [(i, i + 1) for i in range(count - 1)]
    left = [(i + 1, i) for i in range(count - 1)]
    return lax.ppermute(tail, axes, right), lax.ppermute(head, axes, left)


def sum_everywhere(terms):
    axes = ("dp", "expert")
    count = lax.axis_size("dp") * lax.axis_size("expert")
    taps, width = terms.shape
    cells = terms.reshape(count, taps * width // count)
    parts = lax.all_to_all(cells[:, None], axes, 0, 0, tiled=True)
    mine = jnp.sum(parts, axis=0)
    spread = jnp.broadcast_to(mine[None], (count,) + mine.shape)
    return lax.all_to_all(spread, axes, 0, 0, tiled=True).reshape(taps, width)


def body(
    frames,
    cotangent,
    expert_ids,
    conv_weight,
    up_master,
    down_master,
    up_mean_code,
    up_mean_scale,
    up_square_code,
    up_square_scale,
    down_mean_code,
    down_mean_scale,
    down_square_code,
    down_square_scale,
):
    length, width = frames.shape
    taps = conv_weight.shape[0]
    side = taps // 2
    experts = lax.axis_size("expert")
    dp_size = lax.axis_size("dp")
    capacity = 2 * length // experts
    slots = experts * capacity
    hidden = up_master.shape[2]
    rank = lax.axis_index("dp").astype(jnp.int32)
    chip, core, chips = rank // 2, rank % 2, dp_size // 2
    came = [(chip + chips - shift) % chips * 2 for shift in range(chips)]
    goes = [(chip + shift) % chips * 2 for shift in range(chips)]
    order = [base + side_core for base in came for side_core in (core, 1 - core)]
    order = order + [base + side_core for base in goes for side_core in (core, 1 - core)]
    order = jnp.stack(order).astype(jnp.int32)
    product = 2 * slots * width * hidden
    row_shape = ((slots, width), bf16)
    share, depth = hidden // dp_size, width // dp_size

    left, right = halo(frames[:side], frames[length - side :])
    ups, downs = gather_shards(
        *call(
            cast_kernel,
            "cast",
            [],
            [up_master[0], down_master[0]],
            [((share, width), bf16), ((share, width), bf16), ((2 * share, width), bf16)],
            moved=16 * share * width,
        )
    )
    place, send_grads = call(
        functools.partial(dispatch_kernel, experts, capacity),
        "dispatch",
        [],
        [expert_ids.reshape(1, length), cotangent],
        [((slots, length), bf16), row_shape],
        flops=2 * slots * length * width,
        moved=4 * slots * width,
    )
    recv_grads = by_expert(send_grads)
    slope, send_rows = call(
        conv_kernel,
        "convolve",
        [],
        [left, frames, right, conv_weight, place],
        [((length, width), f32), row_shape],
        scratch=[pltpu.VMEM((length + 2 * side, width), f32), pltpu.VMEM((length, width), bf16)],
        flops=2 * slots * length * width,
        moved=8 * slots * width,
    )
    recv_rows = by_expert(send_rows)

    hidden_slope, *down_shares = call(
        functools.partial(forward_kernel, dp_size),
        "forward",
        [order],
        [recv_rows, recv_grads] + ups,
        [((slots, hidden), f32)] + [((chips * share, width), bf16)] * 2,
        scratch=[pltpu.VMEM((slots, hidden), bf16)],
        flops=2 * product,
        moved=4 * width * hidden,
    )
    down_grads = sum_shares(*down_shares)
    grad_pre, back_rows = call(
        functools.partial(backward_kernel, dp_size),
        "backward",
        [order],
        [recv_grads, hidden_slope] + downs + ups,
        [((slots, hidden), bf16), row_shape],
        flops=2 * product,
        moved=4 * width * hidden,
    )
    returned = by_expert(back_rows)
    up_shares = call(
        functools.partial(up_grad_kernel, dp_size),
        "up_grad",
        [order],
        [recv_rows, grad_pre],
        [((chips * depth, hidden), bf16)] * 2,
        flops=product,
        moved=2 * width * hidden,
    )
    up_grads = sum_shares(*up_shares)

    grad_conv, head, tail, conv_terms = call(
        taps_kernel,
        "taps",
        [],
        [place, slope, left, frames, right, returned],
        [((length, width), bf16), ((side, width), bf16), ((side, width), bf16), ((taps, width), f32)],
        scratch=[pltpu.VMEM((length + 2 * side, width), f32)],
        flops=2 * slots * length * width,
        moved=8 * slots * width,
    )
    grad_left, grad_right = halo(head, tail)
    conv_total = sum_everywhere(conv_terms)
    (grad_frames,) = call(
        frames_kernel,
        "frames",
        [],
        [grad_left, grad_conv, grad_right, conv_weight, cotangent],
        [((length, width), bf16)],
        scratch=[pltpu.VMEM((length + 2 * side, width), f32)],
        flops=2 * slots * length * width,
        moved=4 * slots * width,
    )
    down_next = adam(
        "adam_down", down_master, down_grads,
        down_mean_code, down_mean_scale, down_square_code, down_square_scale,
    )
    up_next = adam(
        "adam_up", up_master, up_grads,
        up_mean_code, up_mean_scale, up_square_code, up_square_scale,
    )
    return (grad_frames, conv_total) + up_next + down_next


def solution(mesh):
    frames = P(("dp", "expert"), None)
    shared = P()
    state = P("expert", "dp", None)
    return jax.shard_map(
        body,
        mesh=mesh,
        in_specs=(frames,) * 3 + (shared,) + (state,) * 10,
        out_specs=(frames, shared) + (state,) * 10,
        check_vma=False,
    )
```

```python
import functools

import jax
import jax.numpy as jnp
from jax import lax
from jax.experimental import pallas as pl
from jax.experimental.pallas import tpu as pltpu
from jax.sharding import PartitionSpec as P

beta_one = 0.9
beta_two = 0.95
bias_one = 1.0 - beta_one**10
bias_two = 1.0 - beta_two**10
learn_rate = 0.001
adam_eps = 1e-08
scale_eps = 1e-06

f32 = jnp.float32
bf16 = jnp.bfloat16
MIB = 1 << 20


def swish_parts(values):
    gate_value = jax.nn.sigmoid(values)
    return (values * gate_value, gate_value * (1.0 + values * (1.0 - gate_value)))


def across(lhs, rhs):
    return lax.dot_general(lhs, rhs, (((0,), (0,)), ((), ())), preferred_element_type=f32)


def along(lhs, rhs):
    return lax.dot_general(lhs, rhs, (((1,), (1,)), ((), ())), preferred_element_type=f32)


class Place:
    def __init__(self, dp_size, experts, index_ref):
        index = index_ref[0]
        rank = index // experts
        chips = dp_size // 2
        self.chip, self.core = rank // 2, rank % 2
        self.first = (index > 0).astype(f32)
        self.last = (index < dp_size * experts - 1).astype(f32)
        self.came = [(self.chip + chips - shift) % chips for shift in range(chips)]
        self.goes = [(self.chip + shift) % chips for shift in range(chips)]
        self.shards = [2 * chip + core for chip in self.came for core in (self.core, 1 - self.core)]


def at(block, size):
    return pl.ds(pl.multiple_of(block * size, size), size)


def staged(kernel, counts, spans, *refs):
    groups = []
    for count in counts:
        groups.append(refs[:count])
        refs = refs[count:]
    scalars, sources, _, targets, held, made, scratch = groups
    in_sems, out_sems = refs
    arriving = []
    for index, source in enumerate(sources):
        if spans[index] is not None:
            source = source.at[pl.ds(*spans[index]), :]
        copy = pltpu.make_async_copy(source, held[index], in_sems.at[index])
        copy.start()
        arriving.append(copy)
    leaving = {}

    def take(index):
        if arriving[index] is not None:
            arriving[index].wait()
            arriving[index] = None
        return held[index]

    def give(index):
        leaving[index] = pltpu.make_async_copy(made[index], targets[index], out_sems.at[index])
        leaving[index].start()

    kernel(scalars, take, made, give, scratch)
    for index in range(len(targets)):
        if index not in leaving:
            give(index)
    for index in range(len(sources)):
        take(index)
    for copy in leaving.values():
        copy.wait()


def call(kernel, name, scalars, inputs, outs, scratch=(), after=(), flops=0, moved=0, limit=60):
    hbm = pl.BlockSpec(memory_space=pltpu.HBM)
    smem = pl.BlockSpec(memory_space=pltpu.SMEM)
    pairs = [item if isinstance(item, tuple) else (item, None) for item in inputs]
    arrays = [array for array, _ in pairs]
    spans = [span for _, span in pairs]
    held = [
        pltpu.VMEM(array.shape if span is None else (span[1],) + array.shape[1:], array.dtype)
        for array, span in pairs
    ]
    made = [pltpu.VMEM(shape, kind) for shape, kind in outs]
    counts = (len(scalars), len(arrays), len(after), len(outs), len(held), len(made), len(scratch))
    return pl.pallas_call(
        functools.partial(staged, kernel, counts, spans),
        out_shape=[jax.ShapeDtypeStruct(shape, kind) for shape, kind in outs],
        in_specs=[smem] * len(scalars) + [hbm] * (len(arrays) + len(after)),
        out_specs=[hbm] * len(outs),
        scratch_shapes=held
        + made
        + list(scratch)
        + [pltpu.SemaphoreType.DMA((len(arrays),)), pltpu.SemaphoreType.DMA((len(outs),))],
        compiler_params=pltpu.CompilerParams(vmem_limit_bytes=limit * MIB),
        cost_estimate=pl.CostEstimate(flops=flops, bytes_accessed=moved, transcendentals=0),
        name=name,
    )(*scalars, *arrays, *after)


def dispatch_kernel(experts, capacity, scalars, take, made, give, scratch):
    place_ref, out_ref = made
    ids = take(0)[...]
    length = ids.shape[1]
    rows = lax.broadcasted_iota(jnp.int32, (experts, length), 0)
    one_hot = (rows == ids).astype(f32)
    earlier = lax.broadcasted_iota(jnp.int32, (length, length), 0)
    later = lax.broadcasted_iota(jnp.int32, (length, length), 1)
    ranks = jnp.dot(one_hot, (earlier < later).astype(f32), preferred_element_type=f32)
    slot = jnp.sum(ranks * one_hot, axis=0, keepdims=True).astype(jnp.int32)
    position = ids * capacity + slot
    slots = lax.broadcasted_iota(jnp.int32, (experts * capacity, length), 0)
    place = (slots == position).astype(f32).astype(bf16)
    place_ref[...] = place
    out_ref[...] = jnp.dot(place, take(1)[...], preferred_element_type=f32).astype(bf16)


def fill_padded(pad_ref, place, left, middle, right, cols):
    side, length = left.shape[0], middle.shape[0]
    pad_ref[0:side, :] = left[:, cols].astype(f32) * place.first
    pad_ref[side : side + length, :] = middle[:, cols].astype(f32)
    pad_ref[side + length : side + length + side, :] = right[:, cols].astype(f32) * place.last
    pad_ref[side + length + side :, :] = jnp.zeros((8, pad_ref.shape[1]), f32)


def slide(pad_ref, shift_ref, weights, length):
    total = None
    for rest in range(8):
        part = None
        for tile in range(0, len(weights) - rest, 8):
            if weights[tile + rest] is not None:
                term = weights[tile + rest] * pad_ref[tile : tile + length + 8, :]
                part = term if part is None else part + term
        if rest == 0:
            total = part[:length]
        else:
            shift_ref[: length + 8, :] = part
            total = total + shift_ref[rest : rest + length, :]
    return total


def conv_kernel(here, scalars, take, made, give, scratch):
    slope_ref, out_ref = made
    pad_ref, shift_ref, feat_ref = scratch
    place = here(scalars[0])
    left, frames, right, taps_ref = take(0), take(1), take(2), take(3)
    length, width = feat_ref.shape

    def lanes(step, carry):
        cols = at(step, 128)
        fill_padded(pad_ref, place, left, frames, right, cols)
        weights = [taps_ref[tap : tap + 1, cols] for tap in range(taps_ref.shape[0])]
        active, slope = swish_parts(slide(pad_ref, shift_ref, weights, length))
        slope_ref[:, cols] = slope
        feat_ref[:, cols] = active.astype(bf16)
        return carry

    lax.fori_loop(0, width // 128, lanes, 0)
    give(0)
    out_ref[...] = jnp.dot(take(4)[...], feat_ref[...], preferred_element_type=f32).astype(bf16)


def group_kernel(here, scalars, take, made, give, scratch):
    hidden_ref, pre_ref, part_ref = made
    (slope_ref,) = scratch
    place = here(scalars[0])
    rows_ref = take(0)
    up_refs = [take(1 + shard) for shard in range(len(place.shards))]
    depth = up_refs[0].shape[0]
    units = hidden_ref.shape[1]
    chunk = 256

    def step(index, carry):
        cols = at(index, chunk)
        pre = 0.0
        for shard, up_ref in zip(place.shards, up_refs):
            pre = pre + jnp.dot(
                rows_ref[:, at(shard, depth)], up_ref[:, cols], preferred_element_type=f32
            )
        active, slope = swish_parts(pre)
        hidden_ref[:, cols] = active.astype(bf16)
        slope_ref[:, cols] = slope
        return carry

    lax.fori_loop(0, units // chunk, step, 0, unroll=True)
    give(0)
    grads = take(1 + len(up_refs))[...]
    share = units // 2
    for side, core in enumerate((place.core, 1 - place.core)):
        cols = at(core, share)
        back = along(grads, take(2 + len(up_refs) + side)[...])
        pre_ref[:, cols] = (back * slope_ref[:, cols]).astype(bf16)
    give(1)
    pre = pre_ref[...]
    for shard, up_ref in zip(place.shards, up_refs):
        part_ref[:, at(shard, depth)] = along(pre, up_ref[...]).astype(part_ref.dtype)


def up_grad_kernel(here, groups, scalars, take, made, give, scratch):
    keep_ref, send_ref = made
    place = here(scalars[0])
    row_refs = [take(group) for group in range(groups)]
    pres = [take(groups + group)[...] for group in range(groups)]
    depth = keep_ref.shape[0] // groups
    for out_ref, core in ((send_ref, 1 - place.core), (keep_ref, place.core)):
        for index, chip in enumerate(place.goes):
            total = 0.0
            for row_ref, pre in zip(row_refs, pres):
                total = total + across(row_ref[:, at(2 * chip + core, depth)], pre)
            out_ref[index * depth : (index + 1) * depth, :] = total.astype(bf16)
        give(0 if out_ref is keep_ref else 1)


def down_grad_kernel(here, groups, scalars, take, made, give, scratch):
    keep_ref, send_ref = made
    place = here(scalars[0])
    share = keep_ref.shape[0]
    hidden_refs = [take(group) for group in range(groups)]
    grads = [take(groups + group)[...] for group in range(groups)]
    for out_ref, core in ((send_ref, 1 - place.core), (keep_ref, place.core)):
        total = 0.0
        for hidden_ref, grad in zip(hidden_refs, grads):
            total = total + across(hidden_ref[:, at(core, share)], grad)
        out_ref[...] = total.astype(bf16)
        give(0 if out_ref is keep_ref else 1)


def cast_far_kernel(here, scalars, take, made, give, scratch):
    place = here(scalars[0])
    units = made[0].shape[1]
    for index, up_ref in enumerate(made):
        up_ref[...] = take(0)[:, at(place.goes[index + 1], units)].astype(bf16)
        give(index)


def cast_near_kernel(here, scalars, take, made, give, scratch):
    place = here(scalars[0])
    up_ref, down_ref = made
    up_ref[...] = take(0)[:, at(place.chip, up_ref.shape[1])].astype(bf16)
    give(0)
    down_ref[...] = take(1)[...].astype(bf16)


def taps_kernel(here, scalars, take, made, give, scratch):
    grad_ref, head_ref, tail_ref, terms_ref = made
    pad_ref, shift_ref = scratch
    place = here(scalars[0])
    length, width = grad_ref.shape
    side = head_ref.shape[0]
    features = across(take(0)[...], take(5)[...]).astype(bf16).astype(f32)
    grad = (features * take(1)[...]).astype(bf16)
    grad_ref[...] = grad
    head_ref[...] = grad[:side]
    tail_ref[...] = grad[length - side :]
    give(1)
    give(2)
    give(0)
    left, frames, right = take(2), take(3), take(4)
    shift_ref[0:8, :] = jnp.zeros((8, 128), f32)
    shift_ref[8 + length :, :] = jnp.zeros((8, 128), f32)
    for step in range(width // 128):
        cols = slice(step * 128, (step + 1) * 128)
        fill_padded(pad_ref, place, left, frames, right, cols)
        shift_ref[8 : 8 + length, :] = grad_ref[:, cols].astype(f32)
        for rest in range(8):
            moved = shift_ref[8 - rest : 8 - rest + length + 8, :]
            for tap in range(rest, terms_ref.shape[0], 8):
                product = moved * pad_ref[tap - rest : tap - rest + length + 8, :]
                terms_ref[tap, step : step + 1, :] = jnp.sum(product, axis=0, keepdims=True)


def frames_kernel(here, scalars, take, made, give, scratch):
    (out_ref,) = made
    pad_ref, shift_ref = scratch
    place = here(scalars[0])
    length, width = out_ref.shape
    left, grad, right, taps_ref, cot_ref = take(0), take(1), take(2), take(3), take(4)
    count = taps_ref.shape[0]

    def lanes(step, carry):
        cols = at(step, 128)
        fill_padded(pad_ref, place, left, grad, right, cols)
        weights = [None] + [taps_ref[tap : tap + 1, cols] for tap in range(count - 1, -1, -1)]
        total = slide(pad_ref, shift_ref, weights, length)
        out_ref[:, cols] = (cot_ref[:, cols].astype(f32) + total).astype(bf16)
        return carry

    lax.fori_loop(0, width // 128, lanes, 0)


def adam_kernel(
    here, sums, index_ref, master_ref, mean_ref, mean_scale_ref, square_ref, square_scale_ref, *refs
):
    keep_ref, theirs_ref, far_refs, refs = refs[0], refs[1], refs[2 : 2 + sums], refs[2 + sums :]
    next_ref, mean_next_ref, mean_top_ref, square_next_ref, square_top_ref = refs[:5]
    scales_ref, tops_ref, grad_ref = refs[5:]
    rows, width = master_ref.shape
    blocks = mean_scale_ref.shape[0]
    size = width // blocks
    units = keep_ref.shape[1]
    step = pl.program_id(0)
    steps = pl.num_programs(0)

    @pl.when(step == 0)
    def _():
        scales_ref[0, :, :blocks] = mean_scale_ref[...].T
        scales_ref[1, :, :blocks] = square_scale_ref[...].T

    place = here(index_ref)
    near = slice(0, width) if units == width else at(place.chip, units)
    grad_ref[:, near] = keep_ref[...].astype(f32) + theirs_ref[...].astype(f32)
    for index, far_ref in enumerate(far_refs):
        grad_ref[:, at(place.came[index + 1], units)] = far_ref[...].astype(f32)

    part = at(step, rows)
    mean_scales = scales_ref[0, part, :]
    square_scales = scales_ref[1, part, :]
    for block in range(blocks):
        cols = slice(block * size, (block + 1) * size)
        grad = grad_ref[:, cols]
        mean = beta_one * (
            mean_ref[:, cols].astype(f32) * mean_scales[:, block : block + 1]
        ) + (1.0 - beta_one) * grad
        square = beta_two * (
            square_ref[:, cols].astype(f32) * square_scales[:, block : block + 1]
        ) + (1.0 - beta_two) * (grad * grad)
        root = jnp.sqrt(square * (1.0 / bias_two)) + adam_eps
        next_ref[:, cols] = master_ref[:, cols] - (learn_rate / bias_one) * (mean / root)
        mean_top = jnp.max(jnp.abs(mean), axis=1, keepdims=True) + scale_eps
        square_top = jnp.max(square, axis=1, keepdims=True) + scale_eps
        mean_next_ref[:, cols] = (mean * (1.0 / mean_top)).astype(bf16)
        square_next_ref[:, cols] = (square * (1.0 / square_top)).astype(bf16)
        tops_ref[0, part, block : block + 1] = mean_top
        tops_ref[1, part, block : block + 1] = square_top

    @pl.when(step == steps - 1)
    def _():
        mean_top_ref[...] = tops_ref[0, :, :blocks].T
        square_top_ref[...] = tops_ref[1, :, :blocks].T


def adam(name, here, index, master, grads, mean_code, mean_scale, square_code, square_scale):
    _, rows, width = master.shape
    blocks = mean_scale.shape[-1]
    part = min(rows, (1 << 18) // width)
    tile = pl.BlockSpec((part, width), lambda i: (i, 0))
    whole = pl.BlockSpec((blocks, rows), lambda i: (0, 0))
    pieces = [pl.BlockSpec((part, grad.shape[1]), lambda i: (i, 0)) for grad in grads]
    wide = jax.ShapeDtypeStruct((rows, width), f32)
    code = jax.ShapeDtypeStruct((rows, width), bf16)
    scale = jax.ShapeDtypeStruct((blocks, rows), f32)
    results = pl.pallas_call(
        functools.partial(adam_kernel, here, len(grads) - 2),
        grid=(rows // part,),
        out_shape=[wide, code, scale, code, scale],
        in_specs=[pl.BlockSpec(memory_space=pltpu.SMEM), tile, tile, whole, tile, whole] + pieces,
        out_specs=[tile, tile, whole, tile, whole],
        scratch_shapes=[
            pltpu.VMEM((2, rows, 128), f32),
            pltpu.VMEM((2, rows, 128), f32),
            pltpu.VMEM((part, width), f32),
        ],
        compiler_params=pltpu.CompilerParams(vmem_limit_bytes=60 * MIB),
        cost_estimate=pl.CostEstimate(
            flops=20 * rows * width,
            bytes_accessed=(16 + 2 * len(grads)) * rows * width,
            transcendentals=0,
        ),
        name=name,
    )(index, master[0], mean_code[0], mean_scale[0].T, square_code[0], square_scale[0].T, *grads)
    new_master, mean_next, mean_top, square_next, square_top = results
    return (new_master[None], mean_next[None], mean_top.T[None], square_next[None], square_top.T[None])


def by_expert(rows):
    experts = lax.axis_size("expert")
    slots, width = rows.shape
    cells = rows.reshape(experts, slots // experts, width)
    return lax.all_to_all(cells, "expert", 0, 0, tiled=True).reshape(slots, width)


def to_chip(values, shift):
    count = lax.axis_size("dp")
    chips = count // 2
    return lax.ppermute(
        values, "dp", [(i, (i // 2 + shift) % chips * 2 + i % 2) for i in range(count)]
    )


def to_core(values):
    count = lax.axis_size("dp")
    return lax.ppermute(values, "dp", [(i, i ^ 1) for i in range(count)])


def halo(head, tail):
    axes = ("dp", "expert")
    count = lax.axis_size("dp") * lax.axis_size("expert")
    right = [(i, (i + 1) % count) for i in range(count)]
    left = [((i + 1) % count, i) for i in range(count)]
    return lax.ppermute(tail, axes, right), lax.ppermute(head, axes, left)


def sum_everywhere(terms):
    axes = ("dp", "expert")
    count = lax.axis_size("dp") * lax.axis_size("expert")
    taps, strips, lanes = terms.shape
    cells = terms.reshape(count, taps * strips // count, lanes)
    mine = jnp.sum(lax.all_to_all(cells, axes, 0, 0, tiled=True), axis=0)
    spread = jnp.broadcast_to(mine[None], cells.shape)
    return lax.all_to_all(spread, axes, 0, 0, tiled=True).reshape(taps, strips * lanes)


def body(
    frames,
    cotangent,
    expert_ids,
    conv_weight,
    up_master,
    down_master,
    up_mean_code,
    up_mean_scale,
    up_square_code,
    up_square_scale,
    down_mean_code,
    down_mean_scale,
    down_square_code,
    down_square_scale,
):
    length, width = frames.shape
    taps = conv_weight.shape[0]
    side = taps // 2
    experts = lax.axis_size("expert")
    dp_size = lax.axis_size("dp")
    capacity = 2 * length // experts
    slots = experts * capacity
    hidden = up_master.shape[2]
    chips = dp_size // 2
    index = lax.axis_index("dp") * experts + lax.axis_index("expert")
    index = index.astype(jnp.int32).reshape(1)
    here = functools.partial(Place, dp_size, experts)
    product = 2 * slots * width * hidden // chips
    row_shape = ((slots, width), bf16)
    strips = [pltpu.VMEM((length + 2 * side + 8, 128), f32), pltpu.VMEM((length + 16, 128), f32)]
    share, depth, units = hidden // dp_size, width // dp_size, hidden // chips

    left, right = halo(frames[:side], frames[length - side :])
    up_parts = call(
        functools.partial(cast_far_kernel, here),
        "cast_far",
        [index],
        [up_master[0]],
        [((depth, units), bf16)] * (chips - 1),
        moved=12 * share * width,
    )
    far_ups = [to_chip(part, shift + 1) for shift, part in enumerate(up_parts)]
    up_own, down_own = call(
        functools.partial(cast_near_kernel, here),
        "cast_near",
        [index],
        [up_master[0], down_master[0]],
        [((depth, units), bf16), ((share, width), bf16)],
        after=up_parts[:1],
        moved=12 * share * width,
    )
    ups = [up_own, to_core(up_own)]
    downs = [down_own, to_core(down_own)]
    for arrived in far_ups:
        ups = ups + [arrived, to_core(arrived)]
    place, send_grads = call(
        functools.partial(dispatch_kernel, experts, capacity),
        "dispatch",
        [],
        [expert_ids.reshape(1, length), cotangent],
        [((slots, length), bf16), row_shape],
        after=up_parts[:1],
        flops=2 * slots * length * width,
        moved=4 * slots * width,
    )
    grads_in = by_expert(send_grads)
    slope, send_rows = call(
        functools.partial(conv_kernel, here),
        "convolve",
        [index],
        [left, frames, right, conv_weight, place],
        [((length, width), f32), row_shape],
        after=far_ups,
        scratch=strips + [pltpu.VMEM((length, width), bf16)],
        flops=2 * slots * length * width,
        moved=8 * slots * width,
    )
    rows_in = by_expert(send_rows)

    group_rows = [rows_in] + [to_chip(rows_in, shift) for shift in range(1, chips)]
    group_grads = [grads_in] + [to_chip(grads_in, shift) for shift in range(1, chips)]
    hiddens, pres, parts = [], [], []
    for group in range(chips):
        results = call(
            functools.partial(group_kernel, here),
            "own_group" if group == 0 else "far_group",
            [index],
            [group_rows[group]] + ups + [group_grads[group]] + downs,
            [
                ((slots, units), bf16),
                ((slots, units), bf16),
                ((slots, width), f32 if group == 0 else bf16),
            ],
            scratch=[pltpu.VMEM((slots, units), f32)],
            after=parts[:1],
            flops=3 * product,
            moved=8 * width * units,
        )
        for kind, result in zip((hiddens, pres, parts), results):
            kind.append(result)
    back_total = parts[0]
    for shift in range(1, chips):
        back_total = back_total + to_chip(parts[shift], -shift).astype(f32)
    returned = by_expert(back_total.astype(bf16))
    up_keep, up_send = call(
        functools.partial(up_grad_kernel, here, chips),
        "up_grad",
        [index],
        group_rows + pres,
        [((chips * depth, units), bf16)] * 2,
        flops=chips * product,
        moved=8 * width * units,
    )
    up_theirs = to_core(up_send)
    up_grads = [up_keep, up_theirs]
    for shift in range(1, chips):
        part = slice(shift * depth, (shift + 1) * depth)
        chip_sum = (up_keep[part].astype(f32) + up_theirs[part].astype(f32)).astype(bf16)
        up_grads.append(to_chip(chip_sum, shift))
    down_keep, down_send = call(
        functools.partial(down_grad_kernel, here, chips),
        "down_grad",
        [index],
        hiddens + group_grads,
        [((share, width), bf16)] * 2,
        flops=chips * product,
        moved=8 * width * units,
    )
    down_grads = [down_keep, to_core(down_send)]

    down_next = adam(
        "adam_down", here, index, down_master, down_grads,
        down_mean_code, down_mean_scale, down_square_code, down_square_scale,
    )
    grad_conv, head, tail, conv_terms = call(
        functools.partial(taps_kernel, here),
        "taps",
        [index],
        [place, slope, left, frames, right, returned],
        [((length, width), bf16), ((side, width), bf16), ((side, width), bf16), ((taps, width // 128, 128), f32)],
        after=[down_next[0]],
        scratch=strips,
        flops=2 * slots * length * width,
        moved=8 * slots * width,
    )
    grad_left, grad_right = halo(head, tail)
    conv_total = sum_everywhere(conv_terms)
    (grad_frames,) = call(
        functools.partial(frames_kernel, here),
        "frames",
        [index],
        [grad_left, grad_conv, grad_right, conv_weight, cotangent],
        [((length, width), bf16)],
        scratch=strips,
        flops=2 * slots * length * width,
        moved=4 * slots * width,
    )
    up_next = adam(
        "adam_up", here, index, up_master, up_grads,
        up_mean_code, up_mean_scale, up_square_code, up_square_scale,
    )
    return (grad_frames, conv_total) + up_next + down_next


def solution(mesh):
    frames = P(("dp", "expert"), None)
    shared = P()
    state = P("expert", "dp", None)
    return jax.shard_map(
        body,
        mesh=mesh,
        in_specs=(frames,) * 3 + (shared,) + (state,) * 10,
        out_specs=(frames, shared) + (state,) * 10,
        check_vma=False,
    )
```

```python
import functools
import math

import jax
import jax.numpy as jnp
from jax import lax
from jax.experimental import pallas as pl
from jax.experimental.pallas import tpu as pltpu
from jax.sharding import PartitionSpec as P

beta_one = 0.9
beta_two = 0.95
bias_one = 1.0 - beta_one**10
bias_two = 1.0 - beta_two**10
learn_rate = 0.001
adam_eps = 1e-08
scale_eps = 1e-06

f32 = jnp.float32
bf16 = jnp.bfloat16
MIB = 1 << 20


def swish_parts(values):
    gate_value = jax.nn.sigmoid(values)
    return (values * gate_value, gate_value * (1.0 + values * (1.0 - gate_value)))


def across(lhs, rhs):
    return lax.dot_general(lhs, rhs, (((0,), (0,)), ((), ())), preferred_element_type=f32)


def along(lhs, rhs):
    return lax.dot_general(lhs, rhs, (((1,), (1,)), ((), ())), preferred_element_type=f32)


class Place:
    def __init__(self, dp_size, experts, index_ref):
        index = index_ref[0]
        rank = index // experts
        chips = dp_size // 2
        self.chip, self.core = rank // 2, rank % 2
        self.first = (index > 0).astype(f32)
        self.last = (index < dp_size * experts - 1).astype(f32)
        self.came = [(self.chip + chips - shift) % chips for shift in range(chips)]
        self.goes = [(self.chip + shift) % chips for shift in range(chips)]
        self.shards = [2 * chip + core for chip in self.came for core in (self.core, 1 - self.core)]


def at(block, size):
    return pl.ds(pl.multiple_of(block * size, size), size)


def staged(kernel, counts, spans, *refs):
    groups = []
    for count in counts:
        groups.append(refs[:count])
        refs = refs[count:]
    scalars, resident, sources, _, targets, held, made, scratch = groups
    in_sems, out_sems = refs
    arriving = []
    for index, source in enumerate(sources):
        if spans[index] is not None:
            source = source.at[pl.ds(*spans[index]), :]
        copy = pltpu.make_async_copy(source, held[index], in_sems.at[index])
        copy.start()
        arriving.append(copy)
    leaving = {}

    def take(index):
        if arriving[index] is not None:
            arriving[index].wait()
            arriving[index] = None
        return held[index]

    def give(index):
        leaving[index] = pltpu.make_async_copy(made[index], targets[index], out_sems.at[index])
        leaving[index].start()

    kernel(scalars + resident, take, made, give, scratch)
    for index in range(len(targets)):
        if index not in leaving:
            give(index)
    for index in range(len(sources)):
        take(index)
    for copy in leaving.values():
        copy.wait()


def call(kernel, name, scalars, inputs, outs, scratch=(), after=(), resident=(), flops=0, moved=0, limit=60):
    hbm = pl.BlockSpec(memory_space=pl.ANY)
    vmem = pl.BlockSpec(memory_space=pltpu.VMEM)
    smem = pl.BlockSpec(memory_space=pltpu.SMEM)
    pairs = [item if isinstance(item, tuple) else (item, None) for item in inputs]
    arrays = [array for array, _ in pairs]
    spans = [span for _, span in pairs]
    held = [
        pltpu.VMEM(array.shape if span is None else (span[1],) + array.shape[1:], array.dtype)
        for array, span in pairs
    ]
    made = [pltpu.VMEM(shape, kind) for shape, kind in outs]
    counts = (
        len(scalars), len(resident), len(arrays), len(after), len(outs), len(held), len(made), len(scratch)
    )
    return pl.pallas_call(
        functools.partial(staged, kernel, counts, spans),
        out_shape=[jax.ShapeDtypeStruct(shape, kind) for shape, kind in outs],
        in_specs=[smem] * len(scalars)
        + [vmem] * len(resident)
        + [hbm] * (len(arrays) + len(after)),
        out_specs=[hbm] * len(outs),
        scratch_shapes=held
        + made
        + list(scratch)
        + [pltpu.SemaphoreType.DMA((len(arrays),)), pltpu.SemaphoreType.DMA((len(outs),))],
        compiler_params=pltpu.CompilerParams(vmem_limit_bytes=limit * MIB),
        cost_estimate=pl.CostEstimate(flops=flops, bytes_accessed=moved, transcendentals=0),
        name=name,
    )(*scalars, *resident, *arrays, *after)


def prepare_kernel(here, experts, capacity, scalars, take, made, give, scratch):
    head_ref, tail_ref, place_ref, out_ref, *up_refs = made
    place = here(scalars[0])
    side, length = head_ref.shape[0], place_ref.shape[1]
    frames_ref = take(2)
    head_ref[...] = frames_ref[:side, :]
    give(0)
    tail_ref[...] = frames_ref[length - side :, :]
    give(1)
    ids = take(0)[...]
    rows = lax.broadcasted_iota(jnp.int32, (experts, length), 0)
    one_hot = (rows == ids).astype(f32)
    earlier = lax.broadcasted_iota(jnp.int32, (length, length), 0)
    later = lax.broadcasted_iota(jnp.int32, (length, length), 1)
    ranks = jnp.dot(one_hot, (earlier < later).astype(f32), preferred_element_type=f32)
    slot = jnp.sum(ranks * one_hot, axis=0, keepdims=True).astype(jnp.int32)
    position = ids * capacity + slot
    slots = lax.broadcasted_iota(jnp.int32, (experts * capacity, length), 0)
    spots = (slots == position).astype(f32).astype(bf16)
    place_ref[...] = spots
    give(2)
    out_ref[...] = jnp.dot(spots, take(1)[...], preferred_element_type=f32).astype(bf16)
    give(3)
    units = up_refs[0].shape[1] if up_refs else 0
    for index, up_ref in enumerate(up_refs):
        up_ref[...] = take(3)[:, at(place.goes[index + 1], units)].astype(bf16)
        give(4 + index)


def fill_padded(pad_ref, place, left, middle, right, cols):
    side, length = left.shape[0], middle.shape[0]
    pad_ref[0:side, :] = left[:, cols].astype(f32) * place.first
    pad_ref[side : side + length, :] = middle[:, cols].astype(f32)
    pad_ref[side + length : side + length + side, :] = right[:, cols].astype(f32) * place.last
    pad_ref[side + length + side :, :] = jnp.zeros((8, pad_ref.shape[1]), f32)


def slide(pad_ref, shift_ref, weights, length):
    total = None
    for rest in range(8):
        part = None
        for tile in range(0, len(weights) - rest, 8):
            if weights[tile + rest] is not None:
                term = weights[tile + rest] * pad_ref[tile : tile + length + 8, :]
                part = term if part is None else part + term
        if rest == 0:
            total = part[:length]
        else:
            shift_ref[: length + 8, :] = part
            total = total + shift_ref[rest : rest + length, :]
    return total


def conv_kernel(here, scalars, take, made, give, scratch):
    slope_ref, out_ref = made
    pad_ref, shift_ref, feat_ref = scratch
    place = here(scalars[0])
    left, frames, right, taps_ref = take(0), take(1), take(2), take(3)
    length, width = feat_ref.shape

    def lanes(step, carry):
        cols = at(step, 128)
        fill_padded(pad_ref, place, left, frames, right, cols)
        weights = [taps_ref[tap : tap + 1, cols] for tap in range(taps_ref.shape[0])]
        active, slope = swish_parts(slide(pad_ref, shift_ref, weights, length))
        slope_ref[:, cols] = slope
        feat_ref[:, cols] = active.astype(bf16)
        return carry

    lax.fori_loop(0, width // 128, lanes, 0)
    give(0)
    out_ref[...] = jnp.dot(take(4)[...], feat_ref[...], preferred_element_type=f32).astype(bf16)


def group_kernel(here, others, scalars, take, made, give, scratch):
    hidden_ref, pre_ref, part_ref = made
    (slope_ref,) = scratch
    place = here(scalars[0])
    rows_ref = take(0)
    up_refs = [take(1 + shard) for shard in range(len(place.shards))]
    depth = up_refs[0].shape[0]
    units = hidden_ref.shape[1]
    chunk = 256

    def step(index, carry):
        cols = at(index, chunk)
        pre = 0.0
        for shard, up_ref in zip(place.shards, up_refs):
            pre = pre + jnp.dot(
                rows_ref[:, at(shard, depth)], up_ref[:, cols], preferred_element_type=f32
            )
        active, slope = swish_parts(pre)
        hidden_ref[:, cols] = active.astype(bf16)
        slope_ref[:, cols] = slope
        return carry

    lax.fori_loop(0, units // chunk, step, 0, unroll=True)
    give(0)
    grads = take(1 + len(up_refs))[...]
    share = units // 2
    for side, core in enumerate((place.core, 1 - place.core)):
        cols = at(core, share)
        back = along(grads, take(2 + len(up_refs) + side)[...])
        pre_ref[:, cols] = (back * slope_ref[:, cols]).astype(bf16)
    give(1)
    pre = pre_ref[...]
    spot = slice(None)
    if others:
        slots = rows_ref.shape[0]
        spot = at(place.came[others], slots)
        for turn in range(others):
            part_ref[at(place.came[turn], slots), :] = take(4 + len(up_refs) + turn)[...]
    for shard, up_ref in zip(place.shards, up_refs):
        part_ref[spot, at(shard, depth)] = along(pre, up_ref[...]).astype(bf16)


def up_grad_kernel(here, groups, scalars, take, made, give, scratch):
    keep_ref, send_ref = made
    place = here(scalars[0])
    row_refs = [take(group) for group in range(groups)]
    pres = [take(groups + group)[...] for group in range(groups)]
    depth = keep_ref.shape[0] // len(place.goes)
    for out_ref, core in ((send_ref, 1 - place.core), (keep_ref, place.core)):
        for index, chip in enumerate(place.goes):
            total = 0.0
            for row_ref, pre in zip(row_refs, pres):
                total = total + across(row_ref[:, at(2 * chip + core, depth)], pre)
            out_ref[index * depth : (index + 1) * depth, :] = total.astype(bf16)
        give(0 if out_ref is keep_ref else 1)


def down_grad_kernel(here, groups, scalars, take, made, give, scratch):
    keep_ref, send_ref = made
    place = here(scalars[0])
    share = keep_ref.shape[0]
    hidden_refs = [take(group) for group in range(groups)]
    grads = [take(groups + group)[...] for group in range(groups)]
    for out_ref, core in ((send_ref, 1 - place.core), (keep_ref, place.core)):
        total = 0.0
        for hidden_ref, grad in zip(hidden_refs, grads):
            total = total + across(hidden_ref[:, at(core, share)], grad)
        out_ref[...] = total.astype(bf16)
        give(0 if out_ref is keep_ref else 1)


def cast_near_kernel(here, scalars, take, made, give, scratch):
    place = here(scalars[0])
    up_ref, down_ref = made
    up_ref[...] = take(0)[:, at(place.chip, up_ref.shape[1])].astype(bf16)
    give(0)
    down_ref[...] = take(1)[...].astype(bf16)


def taps_kernel(here, scalars, take, made, give, scratch):
    grad_ref, head_ref, tail_ref, terms_ref = made
    pad_ref, shift_ref = scratch
    place = here(scalars[0])
    length, width = grad_ref.shape
    side = head_ref.shape[0]
    spots, back_ref = take(0)[...], take(5)
    slots = spots.shape[0]
    features = 0.0
    for chip in range(back_ref.shape[0] // slots):
        features = features + across(spots, back_ref[chip * slots : (chip + 1) * slots, :])
    features = features.astype(bf16).astype(f32)
    grad = (features * take(1)[...]).astype(bf16)
    grad_ref[...] = grad
    head_ref[...] = grad[:side]
    tail_ref[...] = grad[length - side :]
    give(1)
    give(2)
    give(0)
    left, frames, right = take(2), take(3), take(4)
    shift_ref[0:8, :] = jnp.zeros((8, 128), f32)
    shift_ref[8 + length :, :] = jnp.zeros((8, 128), f32)
    for step in range(width // 128):
        cols = slice(step * 128, (step + 1) * 128)
        fill_padded(pad_ref, place, left, frames, right, cols)
        shift_ref[8 : 8 + length, :] = grad_ref[:, cols].astype(f32)
        for rest in range(8):
            moved = shift_ref[8 - rest : 8 - rest + length + 8, :]
            for tap in range(rest, terms_ref.shape[0], 8):
                product = moved * pad_ref[tap - rest : tap - rest + length + 8, :]
                terms_ref[tap, step : step + 1, :] = jnp.sum(product, axis=0, keepdims=True)


def frames_kernel(here, scalars, take, made, give, scratch):
    (out_ref,) = made
    pad_ref, shift_ref = scratch
    place = here(scalars[0])
    length, width = out_ref.shape
    left, grad, right, taps_ref, cot_ref = take(0), take(1), take(2), take(3), take(4)
    count = taps_ref.shape[0]

    def lanes(step, carry):
        cols = at(step, 128)
        fill_padded(pad_ref, place, left, grad, right, cols)
        weights = [None] + [taps_ref[tap : tap + 1, cols] for tap in range(count - 1, -1, -1)]
        total = slide(pad_ref, shift_ref, weights, length)
        out_ref[:, cols] = (cot_ref[:, cols].astype(f32) + total).astype(bf16)
        return carry

    lax.fori_loop(0, width // 128, lanes, 0)


def spread_kernel(scalars, take, made, give, scratch):
    total = jnp.sum(take(0)[...], axis=0, keepdims=True)
    made[0][...] = jnp.broadcast_to(total, made[0].shape)


def adam_kernel(
    here, sums, index_ref, master_ref, mean_ref, mean_scale_ref, square_ref, square_scale_ref, *refs
):
    keep_ref, theirs_ref, far_refs, refs = refs[0], refs[1], refs[2 : 2 + sums], refs[2 + sums :]
    next_ref, mean_next_ref, mean_top_ref, square_next_ref, square_top_ref = refs[:5]
    scales_ref, tops_ref, grad_ref = refs[5:]
    rows, width = master_ref.shape
    blocks = mean_scale_ref.shape[0]
    size = width // blocks
    units = keep_ref.shape[1]
    step = pl.program_id(0)
    steps = pl.num_programs(0)

    @pl.when(step == 0)
    def _():
        scales_ref[0, :, :blocks] = mean_scale_ref[...].T
        scales_ref[1, :, :blocks] = square_scale_ref[...].T

    place = here(index_ref)
    near = slice(0, width) if units == width else at(place.chip, units)
    grad_ref[:, near] = keep_ref[...].astype(f32) + theirs_ref[...].astype(f32)
    for index, far_ref in enumerate(far_refs):
        grad_ref[:, at(place.came[index + 1], units)] = far_ref[...].astype(f32)

    part = at(step, rows)
    mean_scales = scales_ref[0, part, :]
    square_scales = scales_ref[1, part, :]
    for block in range(blocks):
        cols = slice(block * size, (block + 1) * size)
        grad = grad_ref[:, cols]
        mean = beta_one * (
            mean_ref[:, cols].astype(f32) * mean_scales[:, block : block + 1]
        ) + (1.0 - beta_one) * grad
        square = beta_two * (
            square_ref[:, cols].astype(f32) * square_scales[:, block : block + 1]
        ) + (1.0 - beta_two) * (grad * grad)
        root = jnp.sqrt(square * (1.0 / bias_two)) + adam_eps
        next_ref[:, cols] = master_ref[:, cols] - (learn_rate / bias_one) * (mean / root)
        mean_top = jnp.max(jnp.abs(mean), axis=1, keepdims=True) + scale_eps
        square_top = jnp.max(square, axis=1, keepdims=True) + scale_eps
        mean_next_ref[:, cols] = (mean * (1.0 / mean_top)).astype(bf16)
        square_next_ref[:, cols] = (square * (1.0 / square_top)).astype(bf16)
        tops_ref[0, part, block : block + 1] = mean_top
        tops_ref[1, part, block : block + 1] = square_top

    @pl.when(step == steps - 1)
    def _():
        mean_top_ref[...] = tops_ref[0, :, :blocks].T
        square_top_ref[...] = tops_ref[1, :, :blocks].T


def adam(name, here, index, master, grads, mean_code, mean_scale, square_code, square_scale):
    _, rows, width = master.shape
    blocks = mean_scale.shape[-1]
    part = min(rows, (1 << 18) // width)
    tile = pl.BlockSpec((part, width), lambda i: (i, 0))
    whole = pl.BlockSpec((blocks, rows), lambda i: (0, 0))
    pieces = [pl.BlockSpec((part, grad.shape[1]), lambda i: (i, 0)) for grad in grads]
    wide = jax.ShapeDtypeStruct((rows, width), f32)
    code = jax.ShapeDtypeStruct((rows, width), bf16)
    scale = jax.ShapeDtypeStruct((blocks, rows), f32)
    results = pl.pallas_call(
        functools.partial(adam_kernel, here, len(grads) - 2),
        grid=(rows // part,),
        out_shape=[wide, code, scale, code, scale],
        in_specs=[pl.BlockSpec(memory_space=pltpu.SMEM), tile, tile, whole, tile, whole] + pieces,
        out_specs=[tile, tile, whole, tile, whole],
        scratch_shapes=[
            pltpu.VMEM((2, rows, 128), f32),
            pltpu.VMEM((2, rows, 128), f32),
            pltpu.VMEM((part, width), f32),
        ],
        compiler_params=pltpu.CompilerParams(vmem_limit_bytes=60 * MIB),
        cost_estimate=pl.CostEstimate(
            flops=20 * rows * width,
            bytes_accessed=(16 + 2 * len(grads)) * rows * width,
            transcendentals=0,
        ),
        name=name,
    )(index, master[0], mean_code[0], mean_scale[0].T, square_code[0], square_scale[0].T, *grads)
    new_master, mean_next, mean_top, square_next, square_top = results
    return (new_master[None], mean_next[None], mean_top.T[None], square_next[None], square_top.T[None])


def by_expert(rows):
    experts = lax.axis_size("expert")
    slots, width = rows.shape
    cells = rows.reshape(experts, slots // experts, width)
    return lax.all_to_all(cells, "expert", 0, 0, tiled=True).reshape(slots, width)


def to_senders(rows):
    axes = ("chip", "expert")
    count = lax.axis_size("chip") * lax.axis_size("expert")
    cells = rows.reshape(count, rows.shape[0] // count, rows.shape[1])
    return lax.all_to_all(cells, axes, 0, 0, tiled=True).reshape(rows.shape)


def to_chip(values, shift):
    chips = lax.axis_size("chip")
    return lax.ppermute(values, "chip", [(i, (i + shift) % chips) for i in range(chips)])


def to_core(values):
    return lax.ppermute(values, "core", [(0, 1), (1, 0)])


def halo(head, tail):
    axes = ("chip", "core", "expert")
    count = math.prod(lax.axis_size(axis) for axis in axes)
    right = [(i, (i + 1) % count) for i in range(count)]
    left = [((i + 1) % count, i) for i in range(count)]
    return lax.ppermute(tail, axes, right), lax.ppermute(head, axes, left)


def sum_everywhere(terms, after):
    axes = ("chip", "core", "expert")
    count = math.prod(lax.axis_size(axis) for axis in axes)
    taps, strips, lanes = terms.shape
    cells = terms.reshape(count, taps * strips // count, lanes)
    parts = lax.all_to_all(cells, axes, 0, 0, tiled=True)
    (spread,) = call(spread_kernel, "spread", [], [parts], [(cells.shape, f32)], after=after)
    return lax.all_to_all(spread, axes, 0, 0, tiled=True).reshape(taps, strips * lanes)


def body(
    frames,
    cotangent,
    expert_ids,
    conv_weight,
    up_master,
    down_master,
    up_mean_code,
    up_mean_scale,
    up_square_code,
    up_square_scale,
    down_mean_code,
    down_mean_scale,
    down_square_code,
    down_square_scale,
):
    length, width = frames.shape
    taps = conv_weight.shape[0]
    side = taps // 2
    experts = lax.axis_size("expert")
    chips = lax.axis_size("chip")
    dp_size = 2 * chips
    capacity = 2 * length // experts
    slots = experts * capacity
    hidden = up_master.shape[2]
    index = lax.axis_index(("chip", "core", "expert"))
    index = index.astype(jnp.int32).reshape(1)
    here = functools.partial(Place, dp_size, experts)
    product = 2 * slots * width * hidden // chips
    row_shape = ((slots, width), bf16)
    strips = [pltpu.VMEM((length + 2 * side + 8, 128), f32), pltpu.VMEM((length + 16, 128), f32)]
    share, depth, units = hidden // dp_size, width // dp_size, hidden // chips

    head, tail, place, send_grads, *up_parts = call(
        functools.partial(prepare_kernel, here, experts, capacity),
        "prepare",
        [index],
        [expert_ids.reshape(1, length), cotangent, frames, up_master[0]],
        [((side, width), bf16)] * 2
        + [((slots, length), bf16), row_shape]
        + [((depth, units), bf16)] * (chips - 1),
        flops=2 * slots * length * width,
        moved=4 * slots * width,
    )
    left, right = halo(head, tail)
    far_ups = [to_chip(part, shift + 1) for shift, part in enumerate(up_parts)]
    up_own, down_own = call(
        functools.partial(cast_near_kernel, here),
        "cast_near",
        [index],
        [up_master[0], down_master[0]],
        [((depth, units), bf16), ((share, width), bf16)],
        after=[place],
        moved=12 * share * width,
    )
    ups = [up_own, to_core(up_own)]
    downs = [down_own, to_core(down_own)]
    for arrived in far_ups:
        ups = ups + [arrived, to_core(arrived)]
    grads_in = by_expert(send_grads)
    slope, send_rows = call(
        functools.partial(conv_kernel, here),
        "convolve",
        [index],
        [left, frames, right, conv_weight, place],
        [((length, width), f32), row_shape],
        after=far_ups + [down_own],
        scratch=strips + [pltpu.VMEM((length, width), bf16)],
        flops=2 * slots * length * width,
        moved=8 * slots * width,
    )
    rows_in = by_expert(send_rows)

    spans = [(rows_in, grads_in)]
    for shift in range(1, chips):
        spans.append((to_chip(rows_in, shift), to_chip(grads_in, shift)))
    hiddens, pres, parts = [], [], []
    for turn, (rows, grads) in enumerate(spans):
        last = turn == chips - 1
        results = call(
            functools.partial(group_kernel, here, turn if last else 0),
            "far_group" if turn else "own_group",
            [index],
            [rows] + ups + [grads] + downs + (parts if last else []),
            [
                ((slots, units), bf16),
                ((slots, units), bf16),
                ((chips * slots if last else slots, width), bf16),
            ],
            scratch=[pltpu.VMEM((slots, units), f32)],
            after=parts[-1:],
            flops=3 * product,
            moved=8 * width * units,
        )
        for kind, result in zip((hiddens, pres, parts), results):
            kind.append(result)
    returned = to_senders(parts[-1])
    group_rows = [rows for rows, _ in spans]
    group_grads = [grads for _, grads in spans]
    up_keep, up_send = call(
        functools.partial(up_grad_kernel, here, len(spans)),
        "up_grad",
        [index],
        group_rows + pres,
        [((chips * depth, units), bf16)] * 2,
        flops=chips * product,
        moved=8 * width * units,
    )
    up_theirs = to_core(up_send)
    up_grads = [up_keep, up_theirs]
    for shift in range(1, chips):
        part = slice(shift * depth, (shift + 1) * depth)
        chip_sum = (up_keep[part].astype(f32) + up_theirs[part].astype(f32)).astype(bf16)
        up_grads.append(to_chip(chip_sum, shift))
    down_keep, down_send = call(
        functools.partial(down_grad_kernel, here, len(spans)),
        "down_grad",
        [index],
        hiddens + group_grads,
        [((share, width), bf16)] * 2,
        flops=chips * product,
        moved=8 * width * units,
    )
    down_grads = [down_keep, to_core(down_send)]

    down_next = adam(
        "adam_down", here, index, down_master, down_grads,
        down_mean_code, down_mean_scale, down_square_code, down_square_scale,
    )
    grad_conv, head, tail, conv_terms = call(
        functools.partial(taps_kernel, here),
        "taps",
        [index],
        [place, slope, left, frames, right, returned],
        [((length, width), bf16), ((side, width), bf16), ((side, width), bf16), ((taps, width // 128, 128), f32)],
        after=[down_next[0]],
        scratch=strips,
        flops=2 * slots * length * width,
        moved=8 * slots * width,
    )
    grad_left, grad_right = halo(head, tail)
    (grad_frames,) = call(
        functools.partial(frames_kernel, here),
        "frames",
        [index],
        [grad_left, grad_conv, grad_right, conv_weight, cotangent],
        [((length, width), bf16)],
        scratch=strips,
        flops=2 * slots * length * width,
        moved=4 * slots * width,
    )
    up_next = adam(
        "adam_up", here, index, up_master, up_grads,
        up_mean_code, up_mean_scale, up_square_code, up_square_scale,
    )
    conv_total = sum_everywhere(conv_terms, [grad_frames])
    return (grad_frames, conv_total) + up_next + down_next


def solution(mesh):
    dp_size, experts = mesh.shape["dp"], mesh.shape["expert"]
    devices = mesh.devices.reshape(dp_size // 2, 2, experts)
    finer = jax.sharding.Mesh(devices, ("chip", "core", "expert"))
    frames = P(("chip", "core", "expert"), None)
    shared = P()
    state = P("expert", ("chip", "core"), None)
    return jax.shard_map(
        body,
        mesh=finer,
        in_specs=(frames,) * 3 + (shared,) + (state,) * 10,
        out_specs=(frames, shared) + (state,) * 10,
        check_vma=False,
    )
```

```python
import functools
import math

import jax
import jax.numpy as jnp
from jax import lax
from jax.experimental import pallas as pl
from jax.experimental.pallas import tpu as pltpu
from jax.sharding import PartitionSpec as P

beta_one = 0.9
beta_two = 0.95
bias_one = 1.0 - beta_one**10
bias_two = 1.0 - beta_two**10
learn_rate = 0.001
adam_eps = 1e-08
scale_eps = 1e-06

f32 = jnp.float32
bf16 = jnp.bfloat16
MIB = 1 << 20


def swish_parts(values):
    gate_value = jax.nn.sigmoid(values)
    return (values * gate_value, gate_value * (1.0 + values * (1.0 - gate_value)))


def across(lhs, rhs):
    return lax.dot_general(lhs, rhs, (((0,), (0,)), ((), ())), preferred_element_type=f32)


def along(lhs, rhs):
    return lax.dot_general(lhs, rhs, (((1,), (1,)), ((), ())), preferred_element_type=f32)


class Place:
    def __init__(self, dp_size, experts, index_ref):
        index = index_ref[0]
        rank = index // experts
        chips = dp_size // 2
        self.chip, self.core = rank // 2, rank % 2
        self.first = (index > 0).astype(f32)
        self.last = (index < dp_size * experts - 1).astype(f32)
        self.came = [(self.chip + chips - shift) % chips for shift in range(chips)]
        self.goes = [(self.chip + shift) % chips for shift in range(chips)]
        self.shards = [2 * chip + core for chip in self.came for core in (self.core, 1 - self.core)]


def at(block, size):
    return pl.ds(pl.multiple_of(block * size, size), size)


def staged(kernel, counts, spans, *refs):
    groups = []
    for count in counts:
        groups.append(refs[:count])
        refs = refs[count:]
    scalars, resident, sources, _, targets, held, made, scratch = groups
    in_sems, out_sems = refs
    arriving = []
    for index, source in enumerate(sources):
        if spans[index] is not None:
            source = source.at[pl.ds(*spans[index]), :]
        copy = pltpu.make_async_copy(source, held[index], in_sems.at[index])
        copy.start()
        arriving.append(copy)
    leaving = {}

    def take(index):
        if arriving[index] is not None:
            arriving[index].wait()
            arriving[index] = None
        return held[index]

    def give(index):
        leaving[index] = pltpu.make_async_copy(made[index], targets[index], out_sems.at[index])
        leaving[index].start()

    kernel(scalars + resident, take, made, give, scratch)
    for index in range(len(targets)):
        if index not in leaving:
            give(index)
    for index in range(len(sources)):
        take(index)
    for copy in leaving.values():
        copy.wait()


def call(kernel, name, scalars, inputs, outs, scratch=(), after=(), resident=(), flops=0, moved=0, limit=63):
    hbm = pl.BlockSpec(memory_space=pl.ANY)
    vmem = pl.BlockSpec(memory_space=pltpu.VMEM)
    smem = pl.BlockSpec(memory_space=pltpu.SMEM)
    pairs = [item if isinstance(item, tuple) else (item, None) for item in inputs]
    arrays = [array for array, _ in pairs]
    spans = [span for _, span in pairs]
    held = [
        pltpu.VMEM(array.shape if span is None else (span[1],) + array.shape[1:], array.dtype)
        for array, span in pairs
    ]
    made = [pltpu.VMEM(shape, kind) for shape, kind in outs]
    counts = (
        len(scalars), len(resident), len(arrays), len(after), len(outs), len(held), len(made), len(scratch)
    )
    return pl.pallas_call(
        functools.partial(staged, kernel, counts, spans),
        out_shape=[jax.ShapeDtypeStruct(shape, kind) for shape, kind in outs],
        in_specs=[smem] * len(scalars)
        + [vmem] * len(resident)
        + [hbm] * (len(arrays) + len(after)),
        out_specs=[hbm] * len(outs),
        scratch_shapes=held
        + made
        + list(scratch)
        + [pltpu.SemaphoreType.DMA((len(arrays),)), pltpu.SemaphoreType.DMA((len(outs),))],
        compiler_params=pltpu.CompilerParams(vmem_limit_bytes=limit * MIB),
        cost_estimate=pl.CostEstimate(flops=flops, bytes_accessed=moved, transcendentals=0),
        name=name,
    )(*scalars, *resident, *arrays, *after)


def prepare_kernel(here, experts, capacity, scalars, take, made, give, scratch):
    head_ref, tail_ref, place_ref, out_ref, *up_refs = made
    place = here(scalars[0])
    side, length = head_ref.shape[0], place_ref.shape[1]
    frames_ref = take(2)
    head_ref[...] = frames_ref[:side, :]
    give(0)
    tail_ref[...] = frames_ref[length - side :, :]
    give(1)
    ids = take(0)[...]
    rows = lax.broadcasted_iota(jnp.int32, (experts, length), 0)
    one_hot = (rows == ids).astype(f32)
    earlier = lax.broadcasted_iota(jnp.int32, (length, length), 0)
    later = lax.broadcasted_iota(jnp.int32, (length, length), 1)
    ranks = jnp.dot(one_hot, (earlier < later).astype(f32), preferred_element_type=f32)
    slot = jnp.sum(ranks * one_hot, axis=0, keepdims=True).astype(jnp.int32)
    position = ids * capacity + slot
    slots = lax.broadcasted_iota(jnp.int32, (experts * capacity, length), 0)
    spots = (slots == position).astype(f32).astype(bf16)
    place_ref[...] = spots
    give(2)
    out_ref[...] = jnp.dot(spots, take(1)[...], preferred_element_type=f32).astype(bf16)
    give(3)
    units = up_refs[0].shape[1] if up_refs else 0
    for index, up_ref in enumerate(up_refs):
        up_ref[...] = take(3)[:, at(place.goes[index + 1], units)].astype(bf16)
        give(4 + index)


def fill_padded(pad_ref, place, left, middle, right, cols):
    side, length = left.shape[0], middle.shape[0]
    pad_ref[0:side, :] = left[:, cols].astype(f32) * place.first
    pad_ref[side : side + length, :] = middle[:, cols].astype(f32)
    pad_ref[side + length : side + length + side, :] = right[:, cols].astype(f32) * place.last
    pad_ref[side + length + side :, :] = jnp.zeros((8, pad_ref.shape[1]), f32)


def slide(pad_ref, shift_ref, weights, length):
    total = None
    for rest in range(8):
        part = None
        for tile in range(0, len(weights) - rest, 8):
            if weights[tile + rest] is not None:
                term = weights[tile + rest] * pad_ref[tile : tile + length + 8, :]
                part = term if part is None else part + term
        if rest == 0:
            total = part[:length]
        else:
            shift_ref[: length + 8, :] = part
            total = total + shift_ref[rest : rest + length, :]
    return total


def conv_kernel(here, scalars, take, made, give, scratch):
    slope_ref, out_ref = made
    pad_ref, shift_ref, feat_ref = scratch
    place = here(scalars[0])
    left, frames, right, taps_ref = take(0), take(1), take(2), take(3)
    length, width = feat_ref.shape

    def lanes(step, carry):
        cols = at(step, 128)
        fill_padded(pad_ref, place, left, frames, right, cols)
        weights = [taps_ref[tap : tap + 1, cols] for tap in range(taps_ref.shape[0])]
        active, slope = swish_parts(slide(pad_ref, shift_ref, weights, length))
        slope_ref[:, cols] = slope
        feat_ref[:, cols] = active.astype(bf16)
        return carry

    lax.fori_loop(0, width // 128, lanes, 0)
    give(0)
    out_ref[...] = jnp.dot(take(4)[...], feat_ref[...], preferred_element_type=f32).astype(bf16)


def group_kernel(here, others, scalars, take, made, give, scratch):
    hidden_ref, pre_ref, part_ref = made
    (slope_ref,) = scratch
    place = here(scalars[0])
    rows_ref = take(0)
    up_refs = [take(1 + shard) for shard in range(len(place.shards))]
    depth = up_refs[0].shape[0]
    units = hidden_ref.shape[1]
    chunk = 256

    def step(index, carry):
        cols = at(index, chunk)
        pre = 0.0
        for shard, up_ref in zip(place.shards, up_refs):
            pre = pre + jnp.dot(
                rows_ref[:, at(shard, depth)], up_ref[:, cols], preferred_element_type=f32
            )
        active, slope = swish_parts(pre)
        hidden_ref[:, cols] = active.astype(bf16)
        slope_ref[:, cols] = slope
        return carry

    lax.fori_loop(0, units // chunk, step, 0, unroll=True)
    give(0)
    grads = take(1 + len(up_refs))[...]
    share = units // 2
    for side, core in enumerate((place.core, 1 - place.core)):
        cols = at(core, share)
        back = along(grads, take(2 + len(up_refs) + side)[...])
        pre_ref[:, cols] = (back * slope_ref[:, cols]).astype(bf16)
    give(1)
    pre = pre_ref[...]
    spot = slice(None)
    if others:
        slots = rows_ref.shape[0]
        spot = at(place.came[others], slots)
        for turn in range(others):
            part_ref[at(place.came[turn], slots), :] = take(4 + len(up_refs) + turn)[...]
    for shard, up_ref in zip(place.shards, up_refs):
        part_ref[spot, at(shard, depth)] = along(pre, up_ref[...]).astype(bf16)


def up_grad_kernel(here, groups, scalars, take, made, give, scratch):
    keep_ref, send_ref = made
    place = here(scalars[0])
    row_refs = [take(group) for group in range(groups)]
    pres = [take(groups + group)[...] for group in range(groups)]
    depth = keep_ref.shape[0] // len(place.goes)
    for out_ref, core in ((send_ref, 1 - place.core), (keep_ref, place.core)):
        for index, chip in enumerate(place.goes):
            total = 0.0
            for row_ref, pre in zip(row_refs, pres):
                total = total + across(row_ref[:, at(2 * chip + core, depth)], pre)
            out_ref[index * depth : (index + 1) * depth, :] = total.astype(bf16)
        give(0 if out_ref is keep_ref else 1)


def down_grad_kernel(here, groups, scalars, take, made, give, scratch):
    keep_ref, send_ref = made
    place = here(scalars[0])
    share = keep_ref.shape[0]
    hidden_refs = [take(group) for group in range(groups)]
    grads = [take(groups + group)[...] for group in range(groups)]
    for out_ref, core in ((send_ref, 1 - place.core), (keep_ref, place.core)):
        total = 0.0
        for hidden_ref, grad in zip(hidden_refs, grads):
            total = total + across(hidden_ref[:, at(core, share)], grad)
        out_ref[...] = total.astype(bf16)
        give(0 if out_ref is keep_ref else 1)


def cast_near_kernel(here, scalars, take, made, give, scratch):
    place = here(scalars[0])
    up_ref, down_ref = made
    up_ref[...] = take(0)[:, at(place.chip, up_ref.shape[1])].astype(bf16)
    give(0)
    down_ref[...] = take(1)[...].astype(bf16)


def taps_kernel(here, scalars, take, made, give, scratch):
    grad_ref, head_ref, tail_ref, terms_ref = made
    pad_ref, shift_ref = scratch
    place = here(scalars[0])
    length, width = grad_ref.shape
    side = head_ref.shape[0]
    spots, back_ref = take(0)[...], take(5)
    slots = spots.shape[0]
    features = 0.0
    for chip in range(back_ref.shape[0] // slots):
        features = features + across(spots, back_ref[chip * slots : (chip + 1) * slots, :])
    features = features.astype(bf16).astype(f32)
    grad = (features * take(1)[...]).astype(bf16)
    grad_ref[...] = grad
    head_ref[...] = grad[:side]
    tail_ref[...] = grad[length - side :]
    give(1)
    give(2)
    give(0)
    left, frames, right = take(2), take(3), take(4)
    shift_ref[0:8, :] = jnp.zeros((8, 128), f32)
    shift_ref[8 + length :, :] = jnp.zeros((8, 128), f32)
    for step in range(width // 128):
        cols = slice(step * 128, (step + 1) * 128)
        fill_padded(pad_ref, place, left, frames, right, cols)
        shift_ref[8 : 8 + length, :] = grad_ref[:, cols].astype(f32)
        for rest in range(8):
            moved = shift_ref[8 - rest : 8 - rest + length + 8, :]
            for tap in range(rest, terms_ref.shape[0], 8):
                product = moved * pad_ref[tap - rest : tap - rest + length + 8, :]
                terms_ref[tap, step : step + 1, :] = jnp.sum(product, axis=0, keepdims=True)


def frames_kernel(here, scalars, take, made, give, scratch):
    (out_ref,) = made
    pad_ref, shift_ref = scratch
    place = here(scalars[0])
    length, width = out_ref.shape
    left, grad, right, taps_ref, cot_ref = take(0), take(1), take(2), take(3), take(4)
    count = taps_ref.shape[0]

    def lanes(step, carry):
        cols = at(step, 128)
        fill_padded(pad_ref, place, left, grad, right, cols)
        weights = [None] + [taps_ref[tap : tap + 1, cols] for tap in range(count - 1, -1, -1)]
        total = slide(pad_ref, shift_ref, weights, length)
        out_ref[:, cols] = (cot_ref[:, cols].astype(f32) + total).astype(bf16)
        return carry

    lax.fori_loop(0, width // 128, lanes, 0)


def spread_kernel(scalars, take, made, give, scratch):
    total = jnp.sum(take(0)[...], axis=0, keepdims=True)
    made[0][...] = jnp.broadcast_to(total, made[0].shape)


def adam_kernel(
    here, sums, index_ref, master_ref, mean_ref, mean_scale_ref, square_ref, square_scale_ref, *refs
):
    keep_ref, theirs_ref, far_refs, refs = refs[0], refs[1], refs[2 : 2 + sums], refs[2 + sums :]
    next_ref, mean_next_ref, mean_top_ref, square_next_ref, square_top_ref = refs[:5]
    scales_ref, tops_ref, grad_ref = refs[5:]
    rows, width = master_ref.shape
    blocks = mean_scale_ref.shape[0]
    size = width // blocks
    units = keep_ref.shape[1]
    step = pl.program_id(0)
    steps = pl.num_programs(0)

    @pl.when(step == 0)
    def _():
        scales_ref[0, :, :blocks] = mean_scale_ref[...].T
        scales_ref[1, :, :blocks] = square_scale_ref[...].T

    place = here(index_ref)
    near = slice(0, width) if units == width else at(place.chip, units)
    grad_ref[:, near] = keep_ref[...].astype(f32) + theirs_ref[...].astype(f32)
    for index, far_ref in enumerate(far_refs):
        grad_ref[:, at(place.came[index + 1], units)] = far_ref[...].astype(f32)

    part = at(step, rows)
    mean_scales = scales_ref[0, part, :]
    square_scales = scales_ref[1, part, :]
    for block in range(blocks):
        cols = slice(block * size, (block + 1) * size)
        grad = grad_ref[:, cols]
        mean = beta_one * (
            mean_ref[:, cols].astype(f32) * mean_scales[:, block : block + 1]
        ) + (1.0 - beta_one) * grad
        square = beta_two * (
            square_ref[:, cols].astype(f32) * square_scales[:, block : block + 1]
        ) + (1.0 - beta_two) * (grad * grad)
        root = jnp.sqrt(square * (1.0 / bias_two)) + adam_eps
        next_ref[:, cols] = master_ref[:, cols] - (learn_rate / bias_one) * (mean / root)
        mean_top = jnp.max(jnp.abs(mean), axis=1, keepdims=True) + scale_eps
        square_top = jnp.max(square, axis=1, keepdims=True) + scale_eps
        mean_next_ref[:, cols] = (mean * (1.0 / mean_top)).astype(bf16)
        square_next_ref[:, cols] = (square * (1.0 / square_top)).astype(bf16)
        tops_ref[0, part, block : block + 1] = mean_top
        tops_ref[1, part, block : block + 1] = square_top

    @pl.when(step == steps - 1)
    def _():
        mean_top_ref[...] = tops_ref[0, :, :blocks].T
        square_top_ref[...] = tops_ref[1, :, :blocks].T


def adam(name, here, index, master, grads, mean_code, mean_scale, square_code, square_scale):
    _, rows, width = master.shape
    blocks = mean_scale.shape[-1]
    part = min(rows, (1 << 18) // width)
    tile = pl.BlockSpec((part, width), lambda i: (i, 0))
    whole = pl.BlockSpec((blocks, rows), lambda i: (0, 0))
    pieces = [pl.BlockSpec((part, grad.shape[1]), lambda i: (i, 0)) for grad in grads]
    wide = jax.ShapeDtypeStruct((rows, width), f32)
    code = jax.ShapeDtypeStruct((rows, width), bf16)
    scale = jax.ShapeDtypeStruct((blocks, rows), f32)
    results = pl.pallas_call(
        functools.partial(adam_kernel, here, len(grads) - 2),
        grid=(rows // part,),
        out_shape=[wide, code, scale, code, scale],
        in_specs=[pl.BlockSpec(memory_space=pltpu.SMEM), tile, tile, whole, tile, whole] + pieces,
        out_specs=[tile, tile, whole, tile, whole],
        scratch_shapes=[
            pltpu.VMEM((2, rows, 128), f32),
            pltpu.VMEM((2, rows, 128), f32),
            pltpu.VMEM((part, width), f32),
        ],
        compiler_params=pltpu.CompilerParams(vmem_limit_bytes=63 * MIB),
        cost_estimate=pl.CostEstimate(
            flops=20 * rows * width,
            bytes_accessed=(16 + 2 * len(grads)) * rows * width,
            transcendentals=0,
        ),
        name=name,
    )(index, master[0], mean_code[0], mean_scale[0].T, square_code[0], square_scale[0].T, *grads)
    new_master, mean_next, mean_top, square_next, square_top = results
    return (new_master[None], mean_next[None], mean_top.T[None], square_next[None], square_top.T[None])


def by_expert(rows):
    experts = lax.axis_size("expert")
    slots, width = rows.shape
    cells = rows.reshape(experts, slots // experts, width)
    return lax.all_to_all(cells, "expert", 0, 0, tiled=True).reshape(slots, width)


def to_senders(rows):
    axes = ("chip", "expert")
    count = lax.axis_size("chip") * lax.axis_size("expert")
    cells = rows.reshape(count, rows.shape[0] // count, rows.shape[1])
    return lax.all_to_all(cells, axes, 0, 0, tiled=True).reshape(rows.shape)


def to_chip(values, shift):
    chips = lax.axis_size("chip")
    return lax.ppermute(values, "chip", [(i, (i + shift) % chips) for i in range(chips)])


def to_core(values):
    return lax.ppermute(values, "core", [(0, 1), (1, 0)])


def halo(head, tail):
    axes = ("chip", "core", "expert")
    count = math.prod(lax.axis_size(axis) for axis in axes)
    right = [(i, (i + 1) % count) for i in range(count)]
    left = [((i + 1) % count, i) for i in range(count)]
    return lax.ppermute(tail, axes, right), lax.ppermute(head, axes, left)


def sum_everywhere(terms, after):
    axes = ("chip", "core", "expert")
    count = math.prod(lax.axis_size(axis) for axis in axes)
    taps, strips, lanes = terms.shape
    cells = terms.reshape(count, taps * strips // count, lanes)
    parts = lax.all_to_all(cells, axes, 0, 0, tiled=True)
    (spread,) = call(spread_kernel, "spread", [], [parts], [(cells.shape, f32)], after=after)
    return lax.all_to_all(spread, axes, 0, 0, tiled=True).reshape(taps, strips * lanes)


def body(
    frames,
    cotangent,
    expert_ids,
    conv_weight,
    up_master,
    down_master,
    up_mean_code,
    up_mean_scale,
    up_square_code,
    up_square_scale,
    down_mean_code,
    down_mean_scale,
    down_square_code,
    down_square_scale,
):
    length, width = frames.shape
    taps = conv_weight.shape[0]
    side = taps // 2
    experts = lax.axis_size("expert")
    chips = lax.axis_size("chip")
    dp_size = 2 * chips
    capacity = 2 * length // experts
    slots = experts * capacity
    hidden = up_master.shape[2]
    index = lax.axis_index(("chip", "core", "expert"))
    index = index.astype(jnp.int32).reshape(1)
    here = functools.partial(Place, dp_size, experts)
    product = 2 * slots * width * hidden // chips
    row_shape = ((slots, width), bf16)
    strips = [pltpu.VMEM((length + 2 * side + 8, 128), f32), pltpu.VMEM((length + 16, 128), f32)]
    share, depth, units = hidden // dp_size, width // dp_size, hidden // chips

    head, tail, place, send_grads, *up_parts = call(
        functools.partial(prepare_kernel, here, experts, capacity),
        "prepare",
        [index],
        [expert_ids.reshape(1, length), cotangent, frames, up_master[0]],
        [((side, width), bf16)] * 2
        + [((slots, length), bf16), row_shape]
        + [((depth, units), bf16)] * (chips - 1),
        flops=2 * slots * length * width,
        moved=4 * slots * width,
    )
    left, right = halo(head, tail)
    far_ups = [to_chip(part, shift + 1) for shift, part in enumerate(up_parts)]
    up_own, down_own = call(
        functools.partial(cast_near_kernel, here),
        "cast_near",
        [index],
        [up_master[0], down_master[0]],
        [((depth, units), bf16), ((share, width), bf16)],
        after=[place],
        moved=12 * share * width,
    )
    ups = [up_own, to_core(up_own)]
    downs = [down_own, to_core(down_own)]
    for arrived in far_ups:
        ups = ups + [arrived, to_core(arrived)]
    grads_in = by_expert(send_grads)
    slope, send_rows = call(
        functools.partial(conv_kernel, here),
        "convolve",
        [index],
        [left, frames, right, conv_weight, place],
        [((length, width), f32), row_shape],
        after=far_ups + [down_own],
        scratch=strips + [pltpu.VMEM((length, width), bf16)],
        flops=2 * slots * length * width,
        moved=8 * slots * width,
    )
    rows_in = by_expert(send_rows)

    spans = [(rows_in, grads_in)]
    for shift in range(1, chips):
        spans.append((to_chip(rows_in, shift), to_chip(grads_in, shift)))
    hiddens, pres, parts = [], [], []
    for turn, (rows, grads) in enumerate(spans):
        last = turn == chips - 1
        results = call(
            functools.partial(group_kernel, here, turn if last else 0),
            "far_group" if turn else "own_group",
            [index],
            [rows] + ups + [grads] + downs + (parts if last else []),
            [
                ((slots, units), bf16),
                ((slots, units), bf16),
                ((chips * slots if last else slots, width), bf16),
            ],
            scratch=[pltpu.VMEM((slots, units), f32)],
            after=parts[-1:],
            flops=3 * product,
            moved=8 * width * units,
        )
        for kind, result in zip((hiddens, pres, parts), results):
            kind.append(result)
    returned = to_senders(parts[-1])
    group_rows = [rows for rows, _ in spans]
    group_grads = [grads for _, grads in spans]
    up_keep, up_send = call(
        functools.partial(up_grad_kernel, here, len(spans)),
        "up_grad",
        [index],
        group_rows + pres,
        [((chips * depth, units), bf16)] * 2,
        flops=chips * product,
        moved=8 * width * units,
    )
    up_theirs = to_core(up_send)
    up_grads = [up_keep, up_theirs]
    for shift in range(1, chips):
        part = slice(shift * depth, (shift + 1) * depth)
        chip_sum = (up_keep[part].astype(f32) + up_theirs[part].astype(f32)).astype(bf16)
        up_grads.append(to_chip(chip_sum, shift))
    down_keep, down_send = call(
        functools.partial(down_grad_kernel, here, len(spans)),
        "down_grad",
        [index],
        hiddens + group_grads,
        [((share, width), bf16)] * 2,
        flops=chips * product,
        moved=8 * width * units,
    )
    down_grads = [down_keep, to_core(down_send)]

    down_next = adam(
        "adam_down", here, index, down_master, down_grads,
        down_mean_code, down_mean_scale, down_square_code, down_square_scale,
    )
    grad_conv, head, tail, conv_terms = call(
        functools.partial(taps_kernel, here),
        "taps",
        [index],
        [place, slope, left, frames, right, returned],
        [((length, width), bf16), ((side, width), bf16), ((side, width), bf16), ((taps, width // 128, 128), f32)],
        after=[down_next[0]],
        scratch=strips,
        flops=2 * slots * length * width,
        moved=8 * slots * width,
    )
    grad_left, grad_right = halo(head, tail)
    (grad_frames,) = call(
        functools.partial(frames_kernel, here),
        "frames",
        [index],
        [grad_left, grad_conv, grad_right, conv_weight, cotangent],
        [((length, width), bf16)],
        scratch=strips,
        flops=2 * slots * length * width,
        moved=4 * slots * width,
    )
    up_next = adam(
        "adam_up", here, index, up_master, up_grads,
        up_mean_code, up_mean_scale, up_square_code, up_square_scale,
    )
    conv_total = sum_everywhere(conv_terms, [up_next[0], grad_left, grad_right])
    return (grad_frames, conv_total) + up_next + down_next


def solution(mesh):
    dp_size, experts = mesh.shape["dp"], mesh.shape["expert"]
    devices = mesh.devices.reshape(dp_size // 2, 2, experts)
    finer = jax.sharding.Mesh(devices, ("chip", "core", "expert"))
    frames = P(("chip", "core", "expert"), None)
    shared = P()
    state = P("expert", ("chip", "core"), None)
    return jax.shard_map(
        body,
        mesh=finer,
        in_specs=(frames,) * 3 + (shared,) + (state,) * 10,
        out_specs=(frames, shared) + (state,) * 10,
        check_vma=False,
    )
```

```python
import functools
import math

import jax
import jax.numpy as jnp
from jax import lax
from jax.experimental import pallas as pl
from jax.experimental.pallas import tpu as pltpu
from jax.sharding import PartitionSpec as P

beta_one = 0.9
beta_two = 0.95
bias_one = 1.0 - beta_one**10
bias_two = 1.0 - beta_two**10
learn_rate = 0.001
adam_eps = 1e-08
scale_eps = 1e-06

f32 = jnp.float32
bf16 = jnp.bfloat16
VMEM_BYTES = 127 << 19


def swish_parts(values):
    gate_value = jax.nn.sigmoid(values)
    return (values * gate_value, gate_value * (1.0 + values * (1.0 - gate_value)))


def across(lhs, rhs):
    return lax.dot_general(lhs, rhs, (((0,), (0,)), ((), ())), preferred_element_type=f32)


def along(lhs, rhs):
    return lax.dot_general(lhs, rhs, (((1,), (1,)), ((), ())), preferred_element_type=f32)


class Place:
    def __init__(self, dp_size, experts, index_ref):
        index = index_ref[0]
        rank = index // experts
        chips = dp_size // 2
        self.chip, self.core = rank // 2, rank % 2
        self.first = (index > 0).astype(f32)
        self.last = (index < dp_size * experts - 1).astype(f32)
        self.came = [(self.chip + chips - shift) % chips for shift in range(chips)]
        self.goes = [(self.chip + shift) % chips for shift in range(chips)]
        self.shards = [2 * chip + core for chip in self.came for core in (self.core, 1 - self.core)]


def at(block, size):
    return pl.ds(pl.multiple_of(block * size, size), size)


def staged(kernel, counts, spans, *refs):
    groups = []
    for count in counts:
        groups.append(refs[:count])
        refs = refs[count:]
    scalars, sources, _, targets, held, made, scratch = groups
    in_sems, out_sems = refs
    arriving = []
    for index, source in enumerate(sources):
        if spans[index] is not None:
            source = source.at[pl.ds(*spans[index]), :]
        copy = pltpu.make_async_copy(source, held[index], in_sems.at[index])
        copy.start()
        arriving.append(copy)
    leaving = {}

    def take(index):
        if arriving[index] is not None:
            arriving[index].wait()
            arriving[index] = None
        return held[index]

    def give(index):
        leaving[index] = pltpu.make_async_copy(made[index], targets[index], out_sems.at[index])
        leaving[index].start()

    kernel(scalars, take, made, give, scratch)
    for index in range(len(targets)):
        if index not in leaving:
            give(index)
    for index in range(len(sources)):
        take(index)
    for copy in leaving.values():
        copy.wait()


def call(kernel, name, scalars, inputs, outs, scratch=(), after=(), flops=0, moved=0):
    hbm = pl.BlockSpec(memory_space=pl.ANY)
    smem = pl.BlockSpec(memory_space=pltpu.SMEM)
    pairs = [item if isinstance(item, tuple) else (item, None) for item in inputs]
    arrays = [array for array, _ in pairs]
    spans = [span for _, span in pairs]
    held = [
        pltpu.VMEM(array.shape if span is None else (span[1],) + array.shape[1:], array.dtype)
        for array, span in pairs
    ]
    made = [pltpu.VMEM(shape, kind) for shape, kind in outs]
    counts = (len(scalars), len(arrays), len(after), len(outs), len(held), len(made), len(scratch))
    return pl.pallas_call(
        functools.partial(staged, kernel, counts, spans),
        out_shape=[jax.ShapeDtypeStruct(shape, kind) for shape, kind in outs],
        in_specs=[smem] * len(scalars)
        + [hbm] * (len(arrays) + len(after)),
        out_specs=[hbm] * len(outs),
        scratch_shapes=held
        + made
        + list(scratch)
        + [pltpu.SemaphoreType.DMA((len(arrays),)), pltpu.SemaphoreType.DMA((len(outs),))],
        compiler_params=pltpu.CompilerParams(vmem_limit_bytes=VMEM_BYTES),
        cost_estimate=pl.CostEstimate(flops=flops, bytes_accessed=moved, transcendentals=0),
        name=name,
    )(*scalars, *arrays, *after)


def prepare_kernel(here, experts, capacity, scalars, take, made, give, scratch):
    head_ref, tail_ref, place_ref, out_ref, *up_refs = made
    place = here(scalars[0])
    side, length = head_ref.shape[0], place_ref.shape[1]
    frames_ref = take(2)
    head_ref[...] = frames_ref[:side, :]
    give(0)
    tail_ref[...] = frames_ref[length - side :, :]
    give(1)
    ids = take(0)[...]
    rows = lax.broadcasted_iota(jnp.int32, (experts, length), 0)
    one_hot = (rows == ids).astype(f32)
    earlier = lax.broadcasted_iota(jnp.int32, (length, length), 0)
    later = lax.broadcasted_iota(jnp.int32, (length, length), 1)
    ranks = jnp.dot(one_hot, (earlier < later).astype(f32), preferred_element_type=f32)
    slot = jnp.sum(ranks * one_hot, axis=0, keepdims=True).astype(jnp.int32)
    position = ids * capacity + slot
    slots = lax.broadcasted_iota(jnp.int32, (experts * capacity, length), 0)
    spots = (slots == position).astype(f32).astype(bf16)
    place_ref[...] = spots
    give(2)
    out_ref[...] = jnp.dot(spots, take(1)[...], preferred_element_type=f32).astype(bf16)
    give(3)
    units = up_refs[0].shape[1] if up_refs else 0
    for index, up_ref in enumerate(up_refs):
        up_ref[...] = take(3)[:, at(place.goes[index + 1], units)].astype(bf16)
        give(4 + index)


def fill_padded(pad_ref, place, left, middle, right, cols):
    side, length = left.shape[0], middle.shape[0]
    pad_ref[0:side, :] = left[:, cols].astype(f32) * place.first
    pad_ref[side : side + length, :] = middle[:, cols].astype(f32)
    pad_ref[side + length : side + length + side, :] = right[:, cols].astype(f32) * place.last
    pad_ref[side + length + side :, :] = jnp.zeros((8, pad_ref.shape[1]), f32)


def slide(pad_ref, shift_ref, weights, length):
    total = None
    for rest in range(8):
        part = None
        for tile in range(0, len(weights) - rest, 8):
            if weights[tile + rest] is not None:
                term = weights[tile + rest] * pad_ref[tile : tile + length + 8, :]
                part = term if part is None else part + term
        if rest == 0:
            total = part[:length]
        else:
            shift_ref[: length + 8, :] = part
            total = total + shift_ref[rest : rest + length, :]
    return total


def conv_kernel(scalars, take, made, give, scratch):
    (total_ref,) = made
    pad_ref, shift_ref = scratch
    frames, taps_ref = take(0), take(1)
    length, width = frames.shape
    side = taps_ref.shape[0] // 2
    pad_ref[:side, :] = jnp.zeros((side, 128), f32)
    pad_ref[side + length :, :] = jnp.zeros((side + 8, 128), f32)

    def lanes(step, carry):
        cols = at(step, 128)
        pad_ref[side : side + length, :] = frames[:, cols].astype(f32)
        weights = [taps_ref[tap : tap + 1, cols] for tap in range(taps_ref.shape[0])]
        total_ref[:, cols] = slide(pad_ref, shift_ref, weights, length)
        return carry

    lax.fori_loop(0, width // 128, lanes, 0)


def edge_kernel(here, scalars, take, made, give, scratch):
    slope_ref, out_ref = made
    pad_ref, shift_ref, feat_ref = scratch
    place = here(scalars[0])
    left, right, total_ref, taps_ref = take(0), take(1), take(2), take(3)
    length, width = feat_ref.shape
    side = left.shape[0]
    count = taps_ref.shape[0]
    pad_ref[: 4 * side + 8, :] = jnp.zeros((4 * side + 8, 128), f32)

    def lanes(step, carry):
        cols = at(step, 128)
        weights = [taps_ref[tap : tap + 1, cols] for tap in range(count)]
        pad_ref[0:side, :] = left[:, cols].astype(f32) * place.first
        head = slide(pad_ref, shift_ref, weights[:side] + [None] * side, side)
        pad_ref[0:side, :] = jnp.zeros((side, 128), f32)
        pad_ref[2 * side : 3 * side, :] = right[:, cols].astype(f32) * place.last
        tail = slide(pad_ref, shift_ref, [None] * (side + 1) + weights[side + 1 :], side)
        pad_ref[2 * side : 3 * side, :] = jnp.zeros((side, 128), f32)
        for rows, extra in (
            (slice(0, side), head),
            (slice(side, length - side), None),
            (slice(length - side, length), tail),
        ):
            total = total_ref[rows, cols]
            if extra is not None:
                total = total + extra
            active, slope = swish_parts(total)
            slope_ref[rows, cols] = slope
            feat_ref[rows, cols] = active.astype(bf16)
        return carry

    lax.fori_loop(0, width // 128, lanes, 0)
    give(0)
    out_ref[...] = jnp.dot(take(4)[...], feat_ref[...], preferred_element_type=f32).astype(bf16)


def group_kernel(here, others, scalars, take, made, give, scratch):
    hidden_ref, pre_ref, part_ref = made
    (slope_ref,) = scratch
    place = here(scalars[0])
    rows_ref = take(0)
    up_refs = [take(1 + shard) for shard in range(len(place.shards))]
    depth = up_refs[0].shape[0]
    units = hidden_ref.shape[1]
    chunk = 256

    def step(index, carry):
        cols = at(index, chunk)
        pre = 0.0
        for shard, up_ref in zip(place.shards, up_refs):
            pre = pre + jnp.dot(
                rows_ref[:, at(shard, depth)], up_ref[:, cols], preferred_element_type=f32
            )
        active, slope = swish_parts(pre)
        hidden_ref[:, cols] = active.astype(bf16)
        slope_ref[:, cols] = slope
        return carry

    lax.fori_loop(0, units // chunk, step, 0, unroll=True)
    give(0)
    grads = take(1 + len(up_refs))[...]
    share = units // 2
    for side, core in enumerate((place.core, 1 - place.core)):
        cols = at(core, share)
        back = along(grads, take(2 + len(up_refs) + side)[...])
        pre_ref[:, cols] = (back * slope_ref[:, cols]).astype(bf16)
    give(1)
    pre = pre_ref[...]
    spot = slice(None)
    if others:
        slots = rows_ref.shape[0]
        spot = at(place.came[others], slots)
        for turn in range(others):
            part_ref[at(place.came[turn], slots), :] = take(4 + len(up_refs) + turn)[...]
    for shard, up_ref in zip(place.shards, up_refs):
        part_ref[spot, at(shard, depth)] = along(pre, up_ref[...]).astype(bf16)


def up_grad_kernel(here, groups, scalars, take, made, give, scratch):
    keep_ref, send_ref = made
    place = here(scalars[0])
    row_refs = [take(group) for group in range(groups)]
    pres = [take(groups + group)[...] for group in range(groups)]
    depth = keep_ref.shape[0] // len(place.goes)
    for out_ref, core in ((send_ref, 1 - place.core), (keep_ref, place.core)):
        for index, chip in enumerate(place.goes):
            total = 0.0
            for row_ref, pre in zip(row_refs, pres):
                total = total + across(row_ref[:, at(2 * chip + core, depth)], pre)
            out_ref[index * depth : (index + 1) * depth, :] = total.astype(bf16)
        give(0 if out_ref is keep_ref else 1)


def down_grad_kernel(here, groups, scalars, take, made, give, scratch):
    keep_ref, send_ref = made
    place = here(scalars[0])
    share = keep_ref.shape[0]
    hidden_refs = [take(group) for group in range(groups)]
    grads = [take(groups + group)[...] for group in range(groups)]
    for out_ref, core in ((send_ref, 1 - place.core), (keep_ref, place.core)):
        total = 0.0
        for hidden_ref, grad in zip(hidden_refs, grads):
            total = total + across(hidden_ref[:, at(core, share)], grad)
        out_ref[...] = total.astype(bf16)
        give(0 if out_ref is keep_ref else 1)


def cast_near_kernel(here, scalars, take, made, give, scratch):
    place = here(scalars[0])
    up_ref, down_ref = made
    up_ref[...] = take(0)[:, at(place.chip, up_ref.shape[1])].astype(bf16)
    give(0)
    down_ref[...] = take(1)[...].astype(bf16)


def taps_kernel(here, scalars, take, made, give, scratch):
    grad_ref, head_ref, tail_ref, terms_ref = made
    pad_ref, shift_ref = scratch
    place = here(scalars[0])
    length, width = grad_ref.shape
    side = head_ref.shape[0]
    spots, back_ref = take(0)[...], take(5)
    slots = spots.shape[0]
    features = 0.0
    for chip in range(back_ref.shape[0] // slots):
        features = features + across(spots, back_ref[chip * slots : (chip + 1) * slots, :])
    features = features.astype(bf16).astype(f32)
    grad = (features * take(1)[...]).astype(bf16)
    grad_ref[...] = grad
    head_ref[...] = grad[:side]
    tail_ref[...] = grad[length - side :]
    give(1)
    give(2)
    give(0)
    left, frames, right = take(2), take(3), take(4)
    shift_ref[0:8, :] = jnp.zeros((8, 128), f32)
    shift_ref[8 + length :, :] = jnp.zeros((8, 128), f32)
    for step in range(width // 128):
        cols = slice(step * 128, (step + 1) * 128)
        fill_padded(pad_ref, place, left, frames, right, cols)
        shift_ref[8 : 8 + length, :] = grad_ref[:, cols].astype(f32)
        for rest in range(8):
            moved = shift_ref[8 - rest : 8 - rest + length + 8, :]
            for tap in range(rest, terms_ref.shape[0], 8):
                product = moved * pad_ref[tap - rest : tap - rest + length + 8, :]
                terms_ref[tap, step : step + 1, :] = jnp.sum(product, axis=0, keepdims=True)


def frames_kernel(here, scalars, take, made, give, scratch):
    (out_ref,) = made
    pad_ref, shift_ref = scratch
    place = here(scalars[0])
    length, width = out_ref.shape
    left, grad, right, taps_ref, cot_ref = take(0), take(1), take(2), take(3), take(4)
    count = taps_ref.shape[0]

    def lanes(step, carry):
        cols = at(step, 128)
        fill_padded(pad_ref, place, left, grad, right, cols)
        weights = [None] + [taps_ref[tap : tap + 1, cols] for tap in range(count - 1, -1, -1)]
        total = slide(pad_ref, shift_ref, weights, length)
        out_ref[:, cols] = (cot_ref[:, cols].astype(f32) + total).astype(bf16)
        return carry

    lax.fori_loop(0, width // 128, lanes, 0)


def spread_kernel(scalars, take, made, give, scratch):
    total = jnp.sum(take(0)[...], axis=0, keepdims=True)
    made[0][...] = jnp.broadcast_to(total, made[0].shape)


def adam_kernel(
    here, sums, index_ref, master_ref, mean_ref, mean_scale_ref, square_ref, square_scale_ref, *refs
):
    keep_ref, theirs_ref, far_refs, refs = refs[0], refs[1], refs[2 : 2 + sums], refs[2 + sums :]
    next_ref, mean_next_ref, mean_top_ref, square_next_ref, square_top_ref = refs[:5]
    split_ref, spread_ref, tops_ref, grad_ref = refs[5:]
    rows, width = master_ref.shape
    blocks = mean_scale_ref.shape[0]
    size = width // blocks
    units = keep_ref.shape[1]
    step = pl.program_id(0)
    steps = pl.num_programs(0)

    @pl.when(step == 0)
    def _():
        lane = lax.broadcasted_iota(jnp.int32, (128, width), 0)
        entry = lax.broadcasted_iota(jnp.int32, (128, width), 1)
        chosen = (lax.rem(lane, blocks) == entry // size) & (lane < 3 * blocks)
        spread_ref[...] = chosen.astype(f32).astype(bf16)
        split_ref[...] = jnp.zeros_like(split_ref)
        for kind, scale_ref in enumerate((mean_scale_ref, square_scale_ref)):
            rest = scale_ref[...]
            for term in range(3):
                piece = rest.astype(bf16).astype(f32)
                split_ref[kind, :, term * blocks : (term + 1) * blocks] = piece.T
                rest = rest - piece

    place = here(index_ref)
    near = slice(0, width) if units == width else at(place.chip, units)
    grad_ref[:, near] = keep_ref[...].astype(f32) + theirs_ref[...].astype(f32)
    for index, far_ref in enumerate(far_refs):
        grad_ref[:, at(place.came[index + 1], units)] = far_ref[...].astype(f32)

    part = at(step, rows)
    mean_scales, square_scales = [
        jnp.dot(
            split_ref[kind, part, :].astype(bf16), spread_ref[...], preferred_element_type=f32
        )
        for kind in range(2)
    ]
    for block in range(blocks):
        cols = slice(block * size, (block + 1) * size)
        grad = grad_ref[:, cols]
        mean = beta_one * (
            mean_ref[:, cols].astype(f32) * mean_scales[:, cols]
        ) + (1.0 - beta_one) * grad
        square = beta_two * (
            square_ref[:, cols].astype(f32) * square_scales[:, cols]
        ) + (1.0 - beta_two) * (grad * grad)
        root = jnp.sqrt(square * (1.0 / bias_two)) + adam_eps
        next_ref[:, cols] = master_ref[:, cols] - (learn_rate / bias_one) * (mean / root)
        mean_top = jnp.max(jnp.abs(mean), axis=1, keepdims=True) + scale_eps
        square_top = jnp.max(square, axis=1, keepdims=True) + scale_eps
        mean_next_ref[:, cols] = (mean * (1.0 / mean_top)).astype(bf16)
        square_next_ref[:, cols] = (square * (1.0 / square_top)).astype(bf16)
        tops_ref[0, part, block : block + 1] = mean_top
        tops_ref[1, part, block : block + 1] = square_top

    @pl.when(step == steps - 1)
    def _():
        mean_top_ref[...] = tops_ref[0, :, :blocks].T
        square_top_ref[...] = tops_ref[1, :, :blocks].T


def adam(name, here, index, master, grads, mean_code, mean_scale, square_code, square_scale):
    _, rows, width = master.shape
    blocks = mean_scale.shape[-1]
    part = min(rows, (1 << 18) // width)
    tile = pl.BlockSpec((part, width), lambda i: (i, 0))
    whole = pl.BlockSpec((blocks, rows), lambda i: (0, 0))
    pieces = [pl.BlockSpec((part, grad.shape[1]), lambda i: (i, 0)) for grad in grads]
    wide = jax.ShapeDtypeStruct((rows, width), f32)
    code = jax.ShapeDtypeStruct((rows, width), bf16)
    scale = jax.ShapeDtypeStruct((blocks, rows), f32)
    results = pl.pallas_call(
        functools.partial(adam_kernel, here, len(grads) - 2),
        grid=(rows // part,),
        out_shape=[wide, code, scale, code, scale],
        in_specs=[pl.BlockSpec(memory_space=pltpu.SMEM), tile, tile, whole, tile, whole] + pieces,
        out_specs=[tile, tile, whole, tile, whole],
        scratch_shapes=[
            pltpu.VMEM((2, rows, 128), f32),
            pltpu.VMEM((128, width), bf16),
            pltpu.VMEM((2, rows, 128), f32),
            pltpu.VMEM((part, width), f32),
        ],
        compiler_params=pltpu.CompilerParams(vmem_limit_bytes=VMEM_BYTES),
        cost_estimate=pl.CostEstimate(
            flops=20 * rows * width,
            bytes_accessed=(16 + 2 * len(grads)) * rows * width,
            transcendentals=0,
        ),
        name=name,
    )(index, master[0], mean_code[0], mean_scale[0].T, square_code[0], square_scale[0].T, *grads)
    new_master, mean_next, mean_top, square_next, square_top = results
    return (new_master[None], mean_next[None], mean_top.T[None], square_next[None], square_top.T[None])


def by_expert(rows):
    experts = lax.axis_size("expert")
    slots, width = rows.shape
    cells = rows.reshape(experts, slots // experts, width)
    return lax.all_to_all(cells, "expert", 0, 0, tiled=True).reshape(slots, width)


def to_senders(rows):
    axes = ("chip", "expert")
    count = lax.axis_size("chip") * lax.axis_size("expert")
    cells = rows.reshape(count, rows.shape[0] // count, rows.shape[1])
    return lax.all_to_all(cells, axes, 0, 0, tiled=True).reshape(rows.shape)


def to_chip(values, shift):
    chips = lax.axis_size("chip")
    return lax.ppermute(values, "chip", [(i, (i + shift) % chips) for i in range(chips)])


def to_core(values):
    return lax.ppermute(values, "core", [(0, 1), (1, 0)])


def halo(head, tail):
    axes = ("chip", "core", "expert")
    count = math.prod(lax.axis_size(axis) for axis in axes)
    right = [(i, (i + 1) % count) for i in range(count)]
    left = [((i + 1) % count, i) for i in range(count)]
    return lax.ppermute(tail, axes, right), lax.ppermute(head, axes, left)


def sum_everywhere(terms, after):
    axes = ("chip", "core", "expert")
    count = math.prod(lax.axis_size(axis) for axis in axes)
    taps, strips, lanes = terms.shape
    cells = terms.reshape(count, taps * strips // count, lanes)
    parts = lax.all_to_all(cells, axes, 0, 0, tiled=True)
    (spread,) = call(spread_kernel, "spread", [], [parts], [(cells.shape, f32)], after=after)
    return lax.all_to_all(spread, axes, 0, 0, tiled=True).reshape(taps, strips * lanes)


def body(
    frames,
    cotangent,
    expert_ids,
    conv_weight,
    up_master,
    down_master,
    up_mean_code,
    up_mean_scale,
    up_square_code,
    up_square_scale,
    down_mean_code,
    down_mean_scale,
    down_square_code,
    down_square_scale,
):
    length, width = frames.shape
    taps = conv_weight.shape[0]
    side = taps // 2
    experts = lax.axis_size("expert")
    chips = lax.axis_size("chip")
    dp_size = 2 * chips
    capacity = 2 * length // experts
    slots = experts * capacity
    hidden = up_master.shape[2]
    index = lax.axis_index(("chip", "core", "expert"))
    index = index.astype(jnp.int32).reshape(1)
    here = functools.partial(Place, dp_size, experts)
    product = 2 * slots * width * hidden // chips
    row_shape = ((slots, width), bf16)
    strips = [pltpu.VMEM((length + 2 * side + 8, 128), f32), pltpu.VMEM((length + 16, 128), f32)]
    share, depth, units = hidden // dp_size, width // dp_size, hidden // chips

    head, tail, place, send_grads, *up_parts = call(
        functools.partial(prepare_kernel, here, experts, capacity),
        "prepare",
        [index],
        [expert_ids.reshape(1, length), cotangent, frames, up_master[0]],
        [((side, width), bf16)] * 2
        + [((slots, length), bf16), row_shape]
        + [((depth, units), bf16)] * (chips - 1),
        flops=2 * slots * length * width,
        moved=4 * slots * width,
    )
    left, right = halo(head, tail)
    far_ups = [to_chip(part, shift + 1) for shift, part in enumerate(up_parts)]
    up_own, down_own = call(
        functools.partial(cast_near_kernel, here),
        "cast_near",
        [index],
        [up_master[0], down_master[0]],
        [((depth, units), bf16), ((share, width), bf16)],
        after=[place],
        moved=12 * share * width,
    )
    ups = [up_own, to_core(up_own)]
    downs = [down_own, to_core(down_own)]
    for arrived in far_ups:
        ups = ups + [arrived, to_core(arrived)]
    grads_in = by_expert(send_grads)
    (inner,) = call(
        conv_kernel,
        "convolve",
        [],
        [frames, conv_weight],
        [((length, width), f32)],
        scratch=strips,
        after=[down_own],
        flops=2 * slots * length * width,
        moved=8 * slots * width,
    )
    slope, send_rows = call(
        functools.partial(edge_kernel, here),
        "edges",
        [index],
        [left, right, inner, conv_weight, place],
        [((length, width), f32), row_shape],
        after=far_ups + [down_own],
        scratch=strips + [pltpu.VMEM((length, width), bf16)],
        flops=2 * slots * length * width,
        moved=8 * slots * width,
    )
    rows_in = by_expert(send_rows)

    spans = [(rows_in, grads_in)]
    for shift in range(1, chips):
        spans.append((to_chip(rows_in, shift), to_chip(grads_in, shift)))
    hiddens, pres, parts = [], [], []
    for turn, (rows, grads) in enumerate(spans):
        last = turn == chips - 1
        results = call(
            functools.partial(group_kernel, here, turn if last else 0),
            "far_group" if turn else "own_group",
            [index],
            [rows] + ups + [grads] + downs + (parts if last else []),
            [
                ((slots, units), bf16),
                ((slots, units), bf16),
                ((chips * slots if last else slots, width), bf16),
            ],
            scratch=[pltpu.VMEM((slots, units), f32)],
            after=parts[-1:],
            flops=3 * product,
            moved=8 * width * units,
        )
        for kind, result in zip((hiddens, pres, parts), results):
            kind.append(result)
    returned = to_senders(parts[-1])
    group_rows = [rows for rows, _ in spans]
    group_grads = [grads for _, grads in spans]
    up_keep, up_send = call(
        functools.partial(up_grad_kernel, here, len(spans)),
        "up_grad",
        [index],
        group_rows + pres,
        [((chips * depth, units), bf16)] * 2,
        flops=chips * product,
        moved=8 * width * units,
    )
    up_theirs = to_core(up_send)
    up_grads = [up_keep, up_theirs]
    for shift in range(1, chips):
        part = slice(shift * depth, (shift + 1) * depth)
        chip_sum = (up_keep[part].astype(f32) + up_theirs[part].astype(f32)).astype(bf16)
        up_grads.append(to_chip(chip_sum, shift))
    down_keep, down_send = call(
        functools.partial(down_grad_kernel, here, len(spans)),
        "down_grad",
        [index],
        hiddens + group_grads,
        [((share, width), bf16)] * 2,
        flops=chips * product,
        moved=8 * width * units,
    )
    down_grads = [down_keep, to_core(down_send)]

    down_next = adam(
        "adam_down", here, index, down_master, down_grads,
        down_mean_code, down_mean_scale, down_square_code, down_square_scale,
    )
    grad_conv, head, tail, conv_terms = call(
        functools.partial(taps_kernel, here),
        "taps",
        [index],
        [place, slope, left, frames, right, returned],
        [((length, width), bf16), ((side, width), bf16), ((side, width), bf16), ((taps, width // 128, 128), f32)],
        after=[down_next[0]],
        scratch=strips,
        flops=2 * slots * length * width,
        moved=8 * slots * width,
    )
    grad_left, grad_right = halo(head, tail)
    (grad_frames,) = call(
        functools.partial(frames_kernel, here),
        "frames",
        [index],
        [grad_left, grad_conv, grad_right, conv_weight, cotangent],
        [((length, width), bf16)],
        scratch=strips,
        flops=2 * slots * length * width,
        moved=4 * slots * width,
    )
    up_next = adam(
        "adam_up", here, index, up_master, up_grads,
        up_mean_code, up_mean_scale, up_square_code, up_square_scale,
    )
    conv_total = sum_everywhere(conv_terms, [up_next[0], grad_left, grad_right])
    return (grad_frames, conv_total) + up_next + down_next


def solution(mesh):
    dp_size, experts = mesh.shape["dp"], mesh.shape["expert"]
    devices = mesh.devices.reshape(dp_size // 2, 2, experts)
    finer = jax.sharding.Mesh(devices, ("chip", "core", "expert"))
    frames = P(("chip", "core", "expert"), None)
    shared = P()
    state = P("expert", ("chip", "core"), None)
    return jax.shard_map(
        body,
        mesh=finer,
        in_specs=(frames,) * 3 + (shared,) + (state,) * 10,
        out_specs=(frames, shared) + (state,) * 10,
        check_vma=False,
    )
```

```python
import functools
import math

import jax
import jax.numpy as jnp
from jax import lax
from jax.experimental import pallas as pl
from jax.experimental.pallas import tpu as pltpu
from jax.sharding import PartitionSpec as P

beta_one = 0.9
beta_two = 0.95
bias_one = 1.0 - beta_one**10
bias_two = 1.0 - beta_two**10
learn_rate = 0.001
adam_eps = 1e-08
scale_eps = 1e-06

f32 = jnp.float32
bf16 = jnp.bfloat16
VMEM_BYTES = 127 << 19


def swish_parts(values):
    gate_value = jax.nn.sigmoid(values)
    return (values * gate_value, gate_value * (1.0 + values * (1.0 - gate_value)))


def across(lhs, rhs):
    return lax.dot_general(lhs, rhs, (((0,), (0,)), ((), ())), preferred_element_type=f32)


def along(lhs, rhs):
    return lax.dot_general(lhs, rhs, (((1,), (1,)), ((), ())), preferred_element_type=f32)


class Place:
    def __init__(self, dp_size, experts, index_ref):
        index = index_ref[0]
        rank = index // experts
        chips = dp_size // 2
        self.chip, self.core = rank // 2, rank % 2
        self.first = (index > 0).astype(f32)
        self.last = (index < dp_size * experts - 1).astype(f32)
        self.came = [(self.chip + chips - shift) % chips for shift in range(chips)]
        self.goes = [(self.chip + shift) % chips for shift in range(chips)]
        self.shards = [2 * chip + core for chip in self.came for core in (self.core, 1 - self.core)]


def at(block, size):
    return pl.ds(pl.multiple_of(block * size, size), size)


def staged(kernel, counts, spans, *refs):
    groups = []
    for count in counts:
        groups.append(refs[:count])
        refs = refs[count:]
    scalars, sources, _, targets, held, made, scratch = groups
    in_sems, out_sems = refs
    arriving = []
    for index, source in enumerate(sources):
        if spans[index] is not None:
            source = source.at[pl.ds(*spans[index]), :]
        copy = pltpu.make_async_copy(source, held[index], in_sems.at[index])
        copy.start()
        arriving.append(copy)
    leaving = {}

    def take(index):
        if arriving[index] is not None:
            arriving[index].wait()
            arriving[index] = None
        return held[index]

    def give(index):
        leaving[index] = pltpu.make_async_copy(made[index], targets[index], out_sems.at[index])
        leaving[index].start()

    kernel(scalars, take, made, give, scratch)
    for index in range(len(targets)):
        if index not in leaving:
            give(index)
    for index in range(len(sources)):
        take(index)
    for copy in leaving.values():
        copy.wait()


def call(kernel, name, scalars, inputs, outs, scratch=(), after=(), flops=0, moved=0):
    hbm = pl.BlockSpec(memory_space=pl.ANY)
    smem = pl.BlockSpec(memory_space=pltpu.SMEM)
    pairs = [item if isinstance(item, tuple) else (item, None) for item in inputs]
    arrays = [array for array, _ in pairs]
    spans = [span for _, span in pairs]
    held = [
        pltpu.VMEM(array.shape if span is None else (span[1],) + array.shape[1:], array.dtype)
        for array, span in pairs
    ]
    made = [pltpu.VMEM(shape, kind) for shape, kind in outs]
    counts = (len(scalars), len(arrays), len(after), len(outs), len(held), len(made), len(scratch))
    return pl.pallas_call(
        functools.partial(staged, kernel, counts, spans),
        out_shape=[jax.ShapeDtypeStruct(shape, kind) for shape, kind in outs],
        in_specs=[smem] * len(scalars)
        + [hbm] * (len(arrays) + len(after)),
        out_specs=[hbm] * len(outs),
        scratch_shapes=held
        + made
        + list(scratch)
        + [pltpu.SemaphoreType.DMA((len(arrays),)), pltpu.SemaphoreType.DMA((len(outs),))],
        compiler_params=pltpu.CompilerParams(vmem_limit_bytes=VMEM_BYTES),
        cost_estimate=pl.CostEstimate(flops=flops, bytes_accessed=moved, transcendentals=0),
        name=name,
    )(*scalars, *arrays, *after)


def prepare_kernel(here, experts, capacity, scalars, take, made, give, scratch):
    head_ref, tail_ref, place_ref, out_ref, *up_refs = made
    place = here(scalars[0])
    side, length = head_ref.shape[0], place_ref.shape[1]
    frames_ref = take(2)
    head_ref[...] = frames_ref[:side, :]
    give(0)
    tail_ref[...] = frames_ref[length - side :, :]
    give(1)
    ids = take(0)[...]
    rows = lax.broadcasted_iota(jnp.int32, (experts, length), 0)
    one_hot = (rows == ids).astype(f32)
    earlier = lax.broadcasted_iota(jnp.int32, (length, length), 0)
    later = lax.broadcasted_iota(jnp.int32, (length, length), 1)
    ranks = jnp.dot(one_hot, (earlier < later).astype(f32), preferred_element_type=f32)
    slot = jnp.sum(ranks * one_hot, axis=0, keepdims=True).astype(jnp.int32)
    position = ids * capacity + slot
    slots = lax.broadcasted_iota(jnp.int32, (experts * capacity, length), 0)
    spots = (slots == position).astype(f32).astype(bf16)
    place_ref[...] = spots
    give(2)
    out_ref[...] = jnp.dot(spots, take(1)[...], preferred_element_type=f32).astype(bf16)
    give(3)
    units = up_refs[0].shape[1] if up_refs else 0
    for index, up_ref in enumerate(up_refs):
        up_ref[...] = take(3)[:, at(place.goes[index + 1], units)].astype(bf16)
        give(4 + index)


def fill_padded(pad_ref, place, left, middle, right, cols):
    side, length = left.shape[0], middle.shape[0]
    pad_ref[0:side, :] = left[:, cols].astype(f32) * place.first
    pad_ref[side : side + length, :] = middle[:, cols].astype(f32)
    pad_ref[side + length : side + length + side, :] = right[:, cols].astype(f32) * place.last
    pad_ref[side + length + side :, :] = jnp.zeros((8, pad_ref.shape[1]), f32)


def slide(pad_ref, shift_ref, weights, length):
    total = None
    for rest in range(8):
        part = None
        for tile in range(0, len(weights) - rest, 8):
            if weights[tile + rest] is not None:
                term = weights[tile + rest] * pad_ref[tile : tile + length + 8, :]
                part = term if part is None else part + term
        if rest == 0:
            total = part[:length]
        else:
            shift_ref[: length + 8, :] = part
            total = total + shift_ref[rest : rest + length, :]
    return total


def conv_kernel(scalars, take, made, give, scratch):
    (total_ref,) = made
    pad_ref, shift_ref = scratch
    frames, taps_ref = take(0), take(1)
    length, width = frames.shape
    side = taps_ref.shape[0] // 2
    pad_ref[:side, :] = jnp.zeros((side, 128), f32)
    pad_ref[side + length :, :] = jnp.zeros((side + 8, 128), f32)

    def lanes(step, carry):
        cols = at(step, 128)
        pad_ref[side : side + length, :] = frames[:, cols].astype(f32)
        weights = [taps_ref[tap : tap + 1, cols] for tap in range(taps_ref.shape[0])]
        total_ref[:, cols] = slide(pad_ref, shift_ref, weights, length)
        return carry

    lax.fori_loop(0, width // 128, lanes, 0)


def edge_kernel(here, scalars, take, made, give, scratch):
    slope_ref, out_ref = made
    pad_ref, shift_ref, feat_ref = scratch
    place = here(scalars[0])
    left, right, total_ref, taps_ref = take(0), take(1), take(2), take(3)
    length, width = feat_ref.shape
    side = left.shape[0]
    count = taps_ref.shape[0]
    pad_ref[: 4 * side + 8, :] = jnp.zeros((4 * side + 8, 128), f32)

    def lanes(step, carry):
        cols = at(step, 128)
        weights = [taps_ref[tap : tap + 1, cols] for tap in range(count)]
        pad_ref[0:side, :] = left[:, cols].astype(f32) * place.first
        head = slide(pad_ref, shift_ref, weights[:side] + [None] * side, side)
        pad_ref[0:side, :] = jnp.zeros((side, 128), f32)
        pad_ref[2 * side : 3 * side, :] = right[:, cols].astype(f32) * place.last
        tail = slide(pad_ref, shift_ref, [None] * (side + 1) + weights[side + 1 :], side)
        pad_ref[2 * side : 3 * side, :] = jnp.zeros((side, 128), f32)
        for rows, extra in (
            (slice(0, side), head),
            (slice(side, length - side), None),
            (slice(length - side, length), tail),
        ):
            total = total_ref[rows, cols]
            if extra is not None:
                total = total + extra
            active, slope = swish_parts(total)
            slope_ref[rows, cols] = slope.astype(bf16)
            feat_ref[rows, cols] = active.astype(bf16)
        return carry

    lax.fori_loop(0, width // 128, lanes, 0)
    give(0)
    out_ref[...] = jnp.dot(take(4)[...], feat_ref[...], preferred_element_type=f32).astype(bf16)


def group_kernel(here, others, scalars, take, made, give, scratch):
    hidden_ref, pre_ref, part_ref = made
    (slope_ref,) = scratch
    place = here(scalars[0])
    rows_ref = take(0)
    up_refs = [take(1 + shard) for shard in range(len(place.shards))]
    depth = up_refs[0].shape[0]
    units = hidden_ref.shape[1]
    chunk = 256

    def step(index, carry):
        cols = at(index, chunk)
        pre = 0.0
        for shard, up_ref in zip(place.shards, up_refs):
            pre = pre + jnp.dot(
                rows_ref[:, at(shard, depth)], up_ref[:, cols], preferred_element_type=f32
            )
        active, slope = swish_parts(pre)
        hidden_ref[:, cols] = active.astype(bf16)
        slope_ref[:, cols] = slope
        return carry

    lax.fori_loop(0, units // chunk, step, 0, unroll=True)
    give(0)
    grads = take(1 + len(up_refs))[...]
    share = units // 2
    for side, core in enumerate((place.core, 1 - place.core)):
        cols = at(core, share)
        back = along(grads, take(2 + len(up_refs) + side)[...])
        pre_ref[:, cols] = (back * slope_ref[:, cols]).astype(bf16)
    give(1)
    pre = pre_ref[...]
    spot = slice(None)
    if others:
        slots = rows_ref.shape[0]
        spot = at(place.came[others], slots)
        for turn in range(others):
            part_ref[at(place.came[turn], slots), :] = take(4 + len(up_refs) + turn)[...]
    for shard, up_ref in zip(place.shards, up_refs):
        part_ref[spot, at(shard, depth)] = along(pre, up_ref[...]).astype(bf16)


def up_grad_kernel(here, groups, scalars, take, made, give, scratch):
    keep_ref, send_ref = made
    place = here(scalars[0])
    row_refs = [take(group) for group in range(groups)]
    pres = [take(groups + group)[...] for group in range(groups)]
    depth = keep_ref.shape[0] // len(place.goes)
    for out_ref, core in ((send_ref, 1 - place.core), (keep_ref, place.core)):
        for index, chip in enumerate(place.goes):
            total = 0.0
            for row_ref, pre in zip(row_refs, pres):
                total = total + across(row_ref[:, at(2 * chip + core, depth)], pre)
            out_ref[index * depth : (index + 1) * depth, :] = total.astype(bf16)
        give(0 if out_ref is keep_ref else 1)


def down_grad_kernel(here, groups, scalars, take, made, give, scratch):
    keep_ref, send_ref = made
    place = here(scalars[0])
    share = keep_ref.shape[0]
    hidden_refs = [take(group) for group in range(groups)]
    grads = [take(groups + group)[...] for group in range(groups)]
    for out_ref, core in ((send_ref, 1 - place.core), (keep_ref, place.core)):
        total = 0.0
        for hidden_ref, grad in zip(hidden_refs, grads):
            total = total + across(hidden_ref[:, at(core, share)], grad)
        out_ref[...] = total.astype(bf16)
        give(0 if out_ref is keep_ref else 1)


def cast_near_kernel(here, scalars, take, made, give, scratch):
    place = here(scalars[0])
    up_ref, down_ref = made
    up_ref[...] = take(0)[:, at(place.chip, up_ref.shape[1])].astype(bf16)
    give(0)
    down_ref[...] = take(1)[...].astype(bf16)


def taps_kernel(here, scalars, take, made, give, scratch):
    grad_ref, head_ref, tail_ref, terms_ref = made
    pad_ref, shift_ref = scratch
    place = here(scalars[0])
    length, width = grad_ref.shape
    side = head_ref.shape[0]
    spots, back_ref = take(0)[...], take(5)
    slots = spots.shape[0]
    features = 0.0
    for chip in range(back_ref.shape[0] // slots):
        features = features + across(spots, back_ref[chip * slots : (chip + 1) * slots, :])
    features = features.astype(bf16).astype(f32)
    grad = (features * take(1)[...].astype(f32)).astype(bf16)
    grad_ref[...] = grad
    head_ref[...] = grad[:side]
    tail_ref[...] = grad[length - side :]
    give(1)
    give(2)
    give(0)
    left, frames, right = take(2), take(3), take(4)
    shift_ref[0:8, :] = jnp.zeros((8, 128), f32)
    shift_ref[8 + length :, :] = jnp.zeros((8, 128), f32)
    strips = width // 128
    for step in range(strips):
        cols = slice(step * 128, (step + 1) * 128)
        fill_padded(pad_ref, place, left, frames, right, cols)
        shift_ref[8 : 8 + length, :] = grad_ref[:, cols].astype(f32)
        for rest in range(8):
            moved = shift_ref[8 - rest : 8 - rest + length + 8, :]
            for tap in range(rest, terms_ref.shape[0] // strips * 8, 8):
                product = moved * pad_ref[tap - rest : tap - rest + length + 8, :]
                tile = tap // 8 * strips + step
                terms_ref[tile, rest : rest + 1, :] = jnp.sum(product, axis=0, keepdims=True)


def frames_kernel(here, scalars, take, made, give, scratch):
    (out_ref,) = made
    pad_ref, shift_ref = scratch
    place = here(scalars[0])
    length, width = out_ref.shape
    left, grad, right, taps_ref, cot_ref = take(0), take(1), take(2), take(3), take(4)
    count = taps_ref.shape[0]

    def lanes(step, carry):
        cols = at(step, 128)
        fill_padded(pad_ref, place, left, grad, right, cols)
        weights = [None] + [taps_ref[tap : tap + 1, cols] for tap in range(count - 1, -1, -1)]
        total = slide(pad_ref, shift_ref, weights, length)
        out_ref[:, cols] = (cot_ref[:, cols].astype(f32) + total).astype(bf16)
        return carry

    lax.fori_loop(0, width // 128, lanes, 0)


def spread_kernel(scalars, take, made, give, scratch):
    total = jnp.sum(take(0)[...], axis=0, keepdims=True)
    made[0][...] = jnp.broadcast_to(total, made[0].shape)


def adam_kernel(
    here, sums, index_ref, master_ref, mean_ref, mean_scale_ref, square_ref, square_scale_ref, *refs
):
    keep_ref, theirs_ref, far_refs, refs = refs[0], refs[1], refs[2 : 2 + sums], refs[2 + sums :]
    next_ref, mean_next_ref, mean_top_ref, square_next_ref, square_top_ref = refs[:5]
    split_ref, spread_ref, tops_ref, grad_ref = refs[5:]
    rows, width = master_ref.shape
    blocks = mean_scale_ref.shape[0]
    size = width // blocks
    units = keep_ref.shape[1]
    step = pl.program_id(0)
    steps = pl.num_programs(0)

    @pl.when(step == 0)
    def _():
        lane = lax.broadcasted_iota(jnp.int32, (128, width), 0)
        entry = lax.broadcasted_iota(jnp.int32, (128, width), 1)
        chosen = (lax.rem(lane, blocks) == entry // size) & (lane < 3 * blocks)
        spread_ref[...] = chosen.astype(f32).astype(bf16)
        split_ref[...] = jnp.zeros_like(split_ref)
        for kind, scale_ref in enumerate((mean_scale_ref, square_scale_ref)):
            rest = scale_ref[...]
            for term in range(3):
                piece = rest.astype(bf16).astype(f32)
                split_ref[kind, :, term * blocks : (term + 1) * blocks] = piece.T
                rest = rest - piece

    place = here(index_ref)
    near = slice(0, width) if units == width else at(place.chip, units)
    grad_ref[:, near] = keep_ref[...].astype(f32) + theirs_ref[...].astype(f32)
    for index, far_ref in enumerate(far_refs):
        grad_ref[:, at(place.came[index + 1], units)] = far_ref[...].astype(f32)

    part = at(step, rows)
    mean_scales, square_scales = [
        jnp.dot(
            split_ref[kind, part, :].astype(bf16), spread_ref[...], preferred_element_type=f32
        )
        for kind in range(2)
    ]
    for block in range(blocks):
        cols = slice(block * size, (block + 1) * size)
        grad = grad_ref[:, cols]
        mean = beta_one * (
            mean_ref[:, cols].astype(f32) * mean_scales[:, cols]
        ) + (1.0 - beta_one) * grad
        square = beta_two * (
            square_ref[:, cols].astype(f32) * square_scales[:, cols]
        ) + (1.0 - beta_two) * (grad * grad)
        root = jnp.sqrt(square * (1.0 / bias_two)) + adam_eps
        next_ref[:, cols] = master_ref[:, cols] - (learn_rate / bias_one) * (mean / root)
        mean_top = jnp.max(jnp.abs(mean), axis=1, keepdims=True) + scale_eps
        square_top = jnp.max(square, axis=1, keepdims=True) + scale_eps
        mean_next_ref[:, cols] = (mean * (1.0 / mean_top)).astype(bf16)
        square_next_ref[:, cols] = (square * (1.0 / square_top)).astype(bf16)
        tops_ref[0, part, block : block + 1] = mean_top
        tops_ref[1, part, block : block + 1] = square_top

    @pl.when(step == steps - 1)
    def _():
        mean_top_ref[...] = tops_ref[0, :, :blocks].T
        square_top_ref[...] = tops_ref[1, :, :blocks].T


def adam(name, here, index, master, grads, mean_code, mean_scale, square_code, square_scale):
    _, rows, width = master.shape
    blocks = mean_scale.shape[-1]
    part = min(rows, (1 << 18) // width)
    tile = pl.BlockSpec((part, width), lambda i: (i, 0))
    whole = pl.BlockSpec((blocks, rows), lambda i: (0, 0))
    pieces = [pl.BlockSpec((part, grad.shape[1]), lambda i: (i, 0)) for grad in grads]
    wide = jax.ShapeDtypeStruct((rows, width), f32)
    code = jax.ShapeDtypeStruct((rows, width), bf16)
    scale = jax.ShapeDtypeStruct((blocks, rows), f32)
    results = pl.pallas_call(
        functools.partial(adam_kernel, here, len(grads) - 2),
        grid=(rows // part,),
        out_shape=[wide, code, scale, code, scale],
        in_specs=[pl.BlockSpec(memory_space=pltpu.SMEM), tile, tile, whole, tile, whole] + pieces,
        out_specs=[tile, tile, whole, tile, whole],
        scratch_shapes=[
            pltpu.VMEM((2, rows, 128), f32),
            pltpu.VMEM((128, width), bf16),
            pltpu.VMEM((2, rows, 128), f32),
            pltpu.VMEM((part, width), f32),
        ],
        compiler_params=pltpu.CompilerParams(vmem_limit_bytes=VMEM_BYTES),
        cost_estimate=pl.CostEstimate(
            flops=20 * rows * width,
            bytes_accessed=(16 + 2 * len(grads)) * rows * width,
            transcendentals=0,
        ),
        name=name,
    )(index, master[0], mean_code[0], mean_scale[0].T, square_code[0], square_scale[0].T, *grads)
    new_master, mean_next, mean_top, square_next, square_top = results
    return (new_master[None], mean_next[None], mean_top.T[None], square_next[None], square_top.T[None])


def by_expert(rows):
    experts = lax.axis_size("expert")
    slots, width = rows.shape
    cells = rows.reshape(experts, slots // experts, width)
    return lax.all_to_all(cells, "expert", 0, 0, tiled=True).reshape(slots, width)


def to_senders(rows):
    axes = ("chip", "expert")
    count = lax.axis_size("chip") * lax.axis_size("expert")
    cells = rows.reshape(count, rows.shape[0] // count, rows.shape[1])
    return lax.all_to_all(cells, axes, 0, 0, tiled=True).reshape(rows.shape)


def to_chip(values, shift):
    chips = lax.axis_size("chip")
    return lax.ppermute(values, "chip", [(i, (i + shift) % chips) for i in range(chips)])


def to_core(values):
    return lax.ppermute(values, "core", [(0, 1), (1, 0)])


def halo(head, tail):
    axes = ("chip", "core", "expert")
    count = math.prod(lax.axis_size(axis) for axis in axes)
    right = [(i, (i + 1) % count) for i in range(count)]
    left = [((i + 1) % count, i) for i in range(count)]
    return lax.ppermute(tail, axes, right), lax.ppermute(head, axes, left)


def sum_everywhere(terms, strips, after):
    axes = ("chip", "core", "expert")
    count = math.prod(lax.axis_size(axis) for axis in axes)
    tiles, rows, lanes = terms.shape
    cells = terms.reshape(count, tiles * rows // count, lanes)
    parts = lax.all_to_all(cells, axes, 0, 0, tiled=True)
    (spread,) = call(spread_kernel, "spread", [], [parts], [(cells.shape, f32)], after=after)
    total = lax.all_to_all(spread, axes, 0, 0, tiled=True)
    total = total.reshape(tiles // strips, strips, rows, lanes).transpose(0, 2, 1, 3)
    return total.reshape(tiles // strips * rows, strips * lanes)


def body(
    frames,
    cotangent,
    expert_ids,
    conv_weight,
    up_master,
    down_master,
    up_mean_code,
    up_mean_scale,
    up_square_code,
    up_square_scale,
    down_mean_code,
    down_mean_scale,
    down_square_code,
    down_square_scale,
):
    length, width = frames.shape
    taps = conv_weight.shape[0]
    side = taps // 2
    experts = lax.axis_size("expert")
    chips = lax.axis_size("chip")
    dp_size = 2 * chips
    capacity = 2 * length // experts
    slots = experts * capacity
    hidden = up_master.shape[2]
    index = lax.axis_index(("chip", "core", "expert"))
    index = index.astype(jnp.int32).reshape(1)
    here = functools.partial(Place, dp_size, experts)
    product = 2 * slots * width * hidden // chips
    row_shape = ((slots, width), bf16)
    strips = [pltpu.VMEM((length + 2 * side + 8, 128), f32), pltpu.VMEM((length + 16, 128), f32)]
    share, depth, units = hidden // dp_size, width // dp_size, hidden // chips

    head, tail, place, send_grads, *up_parts = call(
        functools.partial(prepare_kernel, here, experts, capacity),
        "prepare",
        [index],
        [expert_ids.reshape(1, length), cotangent, frames, up_master[0]],
        [((side, width), bf16)] * 2
        + [((slots, length), bf16), row_shape]
        + [((depth, units), bf16)] * (chips - 1),
        flops=2 * slots * length * width,
        moved=4 * slots * width,
    )
    left, right = halo(head, tail)
    far_ups = [to_chip(part, shift + 1) for shift, part in enumerate(up_parts)]
    up_own, down_own = call(
        functools.partial(cast_near_kernel, here),
        "cast_near",
        [index],
        [up_master[0], down_master[0]],
        [((depth, units), bf16), ((share, width), bf16)],
        after=[place],
        moved=12 * share * width,
    )
    ups = [up_own, to_core(up_own)]
    downs = [down_own, to_core(down_own)]
    for arrived in far_ups:
        ups = ups + [arrived, to_core(arrived)]
    grads_in = by_expert(send_grads)
    (inner,) = call(
        conv_kernel,
        "convolve",
        [],
        [frames, conv_weight],
        [((length, width), f32)],
        scratch=strips,
        after=[down_own],
        flops=2 * slots * length * width,
        moved=8 * slots * width,
    )
    slope, send_rows = call(
        functools.partial(edge_kernel, here),
        "edges",
        [index],
        [left, right, inner, conv_weight, place],
        [((length, width), bf16), row_shape],
        after=far_ups + [down_own],
        scratch=strips + [pltpu.VMEM((length, width), bf16)],
        flops=2 * slots * length * width,
        moved=8 * slots * width,
    )
    rows_in = by_expert(send_rows)

    spans = [(rows_in, grads_in)]
    for shift in range(1, chips):
        spans.append((to_chip(rows_in, shift), to_chip(grads_in, shift)))
    hiddens, pres, parts = [], [], []
    for turn, (rows, grads) in enumerate(spans):
        last = turn == chips - 1
        results = call(
            functools.partial(group_kernel, here, turn if last else 0),
            "far_group" if turn else "own_group",
            [index],
            [rows] + ups + [grads] + downs + (parts if last else []),
            [
                ((slots, units), bf16),
                ((slots, units), bf16),
                ((chips * slots if last else slots, width), bf16),
            ],
            scratch=[pltpu.VMEM((slots, units), f32)],
            after=parts[-1:],
            flops=3 * product,
            moved=8 * width * units,
        )
        for kind, result in zip((hiddens, pres, parts), results):
            kind.append(result)
    returned = to_senders(parts[-1])
    group_rows = [rows for rows, _ in spans]
    group_grads = [grads for _, grads in spans]
    up_keep, up_send = call(
        functools.partial(up_grad_kernel, here, len(spans)),
        "up_grad",
        [index],
        group_rows + pres,
        [((chips * depth, units), bf16)] * 2,
        flops=chips * product,
        moved=8 * width * units,
    )
    up_theirs = to_core(up_send)
    up_grads = [up_keep, up_theirs]
    for shift in range(1, chips):
        part = slice(shift * depth, (shift + 1) * depth)
        chip_sum = (up_keep[part].astype(f32) + up_theirs[part].astype(f32)).astype(bf16)
        up_grads.append(to_chip(chip_sum, shift))
    down_keep, down_send = call(
        functools.partial(down_grad_kernel, here, len(spans)),
        "down_grad",
        [index],
        hiddens + group_grads,
        [((share, width), bf16)] * 2,
        flops=chips * product,
        moved=8 * width * units,
    )
    down_grads = [down_keep, to_core(down_send)]

    down_next = adam(
        "adam_down", here, index, down_master, down_grads,
        down_mean_code, down_mean_scale, down_square_code, down_square_scale,
    )
    grad_conv, head, tail, conv_terms = call(
        functools.partial(taps_kernel, here),
        "taps",
        [index],
        [place, slope, left, frames, right, returned],
        [((length, width), bf16), ((side, width), bf16), ((side, width), bf16), ((taps // 8 * (width // 128), 8, 128), f32)],
        after=[down_next[0]],
        scratch=strips,
        flops=2 * slots * length * width,
        moved=8 * slots * width,
    )
    grad_left, grad_right = halo(head, tail)
    (grad_frames,) = call(
        functools.partial(frames_kernel, here),
        "frames",
        [index],
        [grad_left, grad_conv, grad_right, conv_weight, cotangent],
        [((length, width), bf16)],
        scratch=strips,
        flops=2 * slots * length * width,
        moved=4 * slots * width,
    )
    up_next = adam(
        "adam_up", here, index, up_master, up_grads,
        up_mean_code, up_mean_scale, up_square_code, up_square_scale,
    )
    conv_total = sum_everywhere(conv_terms, width // 128, [up_next[0], grad_left, grad_right])
    return (grad_frames, conv_total) + up_next + down_next


def solution(mesh):
    dp_size, experts = mesh.shape["dp"], mesh.shape["expert"]
    devices = mesh.devices.reshape(dp_size // 2, 2, experts)
    finer = jax.sharding.Mesh(devices, ("chip", "core", "expert"))
    frames = P(("chip", "core", "expert"), None)
    shared = P()
    state = P("expert", ("chip", "core"), None)
    return jax.shard_map(
        body,
        mesh=finer,
        in_specs=(frames,) * 3 + (shared,) + (state,) * 10,
        out_specs=(frames, shared) + (state,) * 10,
        check_vma=False,
    )
```

```python
import functools
import math

import jax
import jax.numpy as jnp
from jax import lax
from jax.experimental import pallas as pl
from jax.experimental.pallas import tpu as pltpu
from jax.sharding import PartitionSpec as P

beta_one = 0.9
beta_two = 0.95
bias_one = 1.0 - beta_one**10
bias_two = 1.0 - beta_two**10
learn_rate = 0.001
adam_eps = 1e-08
scale_eps = 1e-06

f32 = jnp.float32
bf16 = jnp.bfloat16
VMEM_BYTES = 127 << 19


def swish_parts(values):
    gate_value = jax.nn.sigmoid(values)
    return (values * gate_value, gate_value * (1.0 + values * (1.0 - gate_value)))


def across(lhs, rhs):
    return lax.dot_general(lhs, rhs, (((0,), (0,)), ((), ())), preferred_element_type=f32)


def along(lhs, rhs):
    return lax.dot_general(lhs, rhs, (((1,), (1,)), ((), ())), preferred_element_type=f32)


class Place:
    def __init__(self, dp_size, experts, index_ref):
        index = index_ref[0]
        rank = index // experts
        chips = dp_size // 2
        self.chip, self.core = rank // 2, rank % 2
        self.first = (index > 0).astype(f32)
        self.last = (index < dp_size * experts - 1).astype(f32)
        self.came = [(self.chip + chips - shift) % chips for shift in range(chips)]
        self.goes = [(self.chip + shift) % chips for shift in range(chips)]
        self.shards = [2 * chip + core for chip in self.came for core in (self.core, 1 - self.core)]


def at(block, size):
    return pl.ds(pl.multiple_of(block * size, size), size)


def staged(kernel, counts, spans, *refs):
    groups = []
    for count in counts:
        groups.append(refs[:count])
        refs = refs[count:]
    scalars, sources, _, targets, held, made, scratch = groups
    in_sems, out_sems = refs
    arriving = []
    for index, source in enumerate(sources):
        if spans[index] is not None:
            source = source.at[pl.ds(*spans[index]), :]
        copy = pltpu.make_async_copy(source, held[index], in_sems.at[index])
        copy.start()
        arriving.append(copy)
    leaving = {}

    def take(index):
        if arriving[index] is not None:
            arriving[index].wait()
            arriving[index] = None
        return held[index]

    def give(index):
        leaving[index] = pltpu.make_async_copy(made[index], targets[index], out_sems.at[index])
        leaving[index].start()

    kernel(scalars, take, made, give, scratch)
    for index in range(len(targets)):
        if index not in leaving:
            give(index)
    for index in range(len(sources)):
        take(index)
    for copy in leaving.values():
        copy.wait()


def call(kernel, name, scalars, inputs, outs, scratch=(), after=(), flops=0, moved=0):
    hbm = pl.BlockSpec(memory_space=pl.ANY)
    smem = pl.BlockSpec(memory_space=pltpu.SMEM)
    pairs = [item if isinstance(item, tuple) else (item, None) for item in inputs]
    arrays = [array for array, _ in pairs]
    spans = [span for _, span in pairs]
    held = [
        pltpu.VMEM(array.shape if span is None else (span[1],) + array.shape[1:], array.dtype)
        for array, span in pairs
    ]
    made = [pltpu.VMEM(shape, kind) for shape, kind in outs]
    counts = (len(scalars), len(arrays), len(after), len(outs), len(held), len(made), len(scratch))
    return pl.pallas_call(
        functools.partial(staged, kernel, counts, spans),
        out_shape=[jax.ShapeDtypeStruct(shape, kind) for shape, kind in outs],
        in_specs=[smem] * len(scalars)
        + [hbm] * (len(arrays) + len(after)),
        out_specs=[hbm] * len(outs),
        scratch_shapes=held
        + made
        + list(scratch)
        + [pltpu.SemaphoreType.DMA((len(arrays),)), pltpu.SemaphoreType.DMA((len(outs),))],
        compiler_params=pltpu.CompilerParams(vmem_limit_bytes=VMEM_BYTES),
        cost_estimate=pl.CostEstimate(flops=flops, bytes_accessed=moved, transcendentals=0),
        name=name,
    )(*scalars, *arrays, *after)


def prepare_kernel(here, experts, capacity, scalars, take, made, give, scratch):
    head_ref, tail_ref, place_ref, out_ref, *up_refs = made
    place = here(scalars[0])
    side, length = head_ref.shape[0], place_ref.shape[1]
    frames_ref = take(2)
    head_ref[...] = frames_ref[:side, :]
    give(0)
    tail_ref[...] = frames_ref[length - side :, :]
    give(1)
    ids = take(0)[...]
    rows = lax.broadcasted_iota(jnp.int32, (experts, length), 0)
    one_hot = (rows == ids).astype(f32)
    earlier = lax.broadcasted_iota(jnp.int32, (length, length), 0)
    later = lax.broadcasted_iota(jnp.int32, (length, length), 1)
    ranks = jnp.dot(one_hot, (earlier < later).astype(f32), preferred_element_type=f32)
    slot = jnp.sum(ranks * one_hot, axis=0, keepdims=True).astype(jnp.int32)
    position = ids * capacity + slot
    slots = lax.broadcasted_iota(jnp.int32, (experts * capacity, length), 0)
    spots = (slots == position).astype(f32).astype(bf16)
    place_ref[...] = spots
    give(2)
    out_ref[...] = jnp.dot(spots, take(1)[...], preferred_element_type=f32).astype(bf16)
    give(3)
    units = up_refs[0].shape[1] if up_refs else 0
    for index, up_ref in enumerate(up_refs):
        up_ref[...] = take(3)[:, at(place.goes[index + 1], units)].astype(bf16)
        give(4 + index)


def fill_padded(pad_ref, place, left, middle, right, cols):
    side, length = left.shape[0], middle.shape[0]
    pad_ref[0:side, :] = left[:, cols].astype(f32) * place.first
    pad_ref[side : side + length, :] = middle[:, cols].astype(f32)
    pad_ref[side + length : side + length + side, :] = right[:, cols].astype(f32) * place.last
    pad_ref[side + length + side :, :] = jnp.zeros((8, pad_ref.shape[1]), f32)


def slide(pad_ref, shift_ref, weights, length):
    total = None
    for rest in range(8):
        part = None
        for tile in range(0, len(weights) - rest, 8):
            if weights[tile + rest] is not None:
                term = weights[tile + rest] * pad_ref[tile : tile + length + 8, :]
                part = term if part is None else part + term
        if rest == 0:
            total = part[:length]
        else:
            shift_ref[: length + 8, :] = part
            total = total + shift_ref[rest : rest + length, :]
    return total


def conv_kernel(scalars, take, made, give, scratch):
    (total_ref,) = made
    pad_ref, shift_ref = scratch
    frames, taps_ref = take(0), take(1)
    length, width = frames.shape
    side = taps_ref.shape[0] // 2
    pad_ref[:side, :] = jnp.zeros((side, 128), f32)
    pad_ref[side + length :, :] = jnp.zeros((side + 8, 128), f32)

    def lanes(step, carry):
        cols = at(step, 128)
        pad_ref[side : side + length, :] = frames[:, cols].astype(f32)
        weights = [taps_ref[tap : tap + 1, cols] for tap in range(taps_ref.shape[0])]
        total_ref[:, cols] = slide(pad_ref, shift_ref, weights, length)
        return carry

    lax.fori_loop(0, width // 128, lanes, 0)


def edge_kernel(here, scalars, take, made, give, scratch):
    slope_ref, out_ref = made
    pad_ref, shift_ref, feat_ref = scratch
    place = here(scalars[0])
    left, right, total_ref, taps_ref = take(0), take(1), take(2), take(3)
    length, width = feat_ref.shape
    side = left.shape[0]
    count = taps_ref.shape[0]
    pad_ref[: 4 * side + 8, :] = jnp.zeros((4 * side + 8, 128), f32)

    def lanes(step, carry):
        cols = at(step, 128)
        weights = [taps_ref[tap : tap + 1, cols] for tap in range(count)]
        pad_ref[0:side, :] = left[:, cols].astype(f32) * place.first
        head = slide(pad_ref, shift_ref, weights[:side] + [None] * side, side)
        pad_ref[0:side, :] = jnp.zeros((side, 128), f32)
        pad_ref[2 * side : 3 * side, :] = right[:, cols].astype(f32) * place.last
        tail = slide(pad_ref, shift_ref, [None] * (side + 1) + weights[side + 1 :], side)
        pad_ref[2 * side : 3 * side, :] = jnp.zeros((side, 128), f32)
        for rows, extra in (
            (slice(0, side), head),
            (slice(side, length - side), None),
            (slice(length - side, length), tail),
        ):
            total = total_ref[rows, cols]
            if extra is not None:
                total = total + extra
            active, slope = swish_parts(total)
            slope_ref[rows, cols] = slope.astype(bf16)
            feat_ref[rows, cols] = active.astype(bf16)
        return carry

    lax.fori_loop(0, width // 128, lanes, 0)
    give(0)
    out_ref[...] = jnp.dot(take(4)[...], feat_ref[...], preferred_element_type=f32).astype(bf16)


def group_kernel(here, others, scalars, take, made, give, scratch):
    hidden_ref, pre_ref, part_ref = made
    (slope_ref,) = scratch
    place = here(scalars[0])
    rows_ref = take(0)
    up_refs = [take(1 + shard) for shard in range(len(place.shards))]
    depth = up_refs[0].shape[0]
    units = hidden_ref.shape[1]
    chunk = 512

    def step(index, carry):
        cols = at(index, chunk)
        pre = 0.0
        for shard, up_ref in zip(place.shards, up_refs):
            pre = pre + jnp.dot(
                rows_ref[:, at(shard, depth)], up_ref[:, cols], preferred_element_type=f32
            )
        active, slope = swish_parts(pre)
        hidden_ref[:, cols] = active.astype(bf16)
        slope_ref[:, cols] = slope
        return carry

    lax.fori_loop(0, units // chunk, step, 0, unroll=True)
    give(0)
    grads = take(1 + len(up_refs))[...]
    share = units // 2
    for side, core in enumerate((place.core, 1 - place.core)):
        cols = at(core, share)
        back = along(grads, take(2 + len(up_refs) + side)[...])
        pre_ref[:, cols] = (back * slope_ref[:, cols]).astype(bf16)
    give(1)
    pre = pre_ref[...]
    spot = slice(None)
    if others:
        slots = rows_ref.shape[0]
        spot = at(place.came[others], slots)
        for turn in range(others):
            part_ref[at(place.came[turn], slots), :] = take(4 + len(up_refs) + turn)[...]
    for shard, up_ref in zip(place.shards, up_refs):
        part_ref[spot, at(shard, depth)] = along(pre, up_ref[...]).astype(bf16)


def up_grad_kernel(here, groups, scalars, take, made, give, scratch):
    keep_ref, send_ref = made
    place = here(scalars[0])
    row_refs = [take(group) for group in range(groups)]
    pres = [take(groups + group)[...] for group in range(groups)]
    depth = keep_ref.shape[0] // len(place.goes)
    for out_ref, core in ((send_ref, 1 - place.core), (keep_ref, place.core)):
        for index, chip in enumerate(place.goes):
            total = 0.0
            for row_ref, pre in zip(row_refs, pres):
                total = total + across(row_ref[:, at(2 * chip + core, depth)], pre)
            out_ref[index * depth : (index + 1) * depth, :] = total.astype(bf16)
        give(0 if out_ref is keep_ref else 1)


def down_grad_kernel(here, groups, scalars, take, made, give, scratch):
    keep_ref, send_ref = made
    place = here(scalars[0])
    share = keep_ref.shape[0]
    hidden_refs = [take(group) for group in range(groups)]
    grads = [take(groups + group)[...] for group in range(groups)]
    for out_ref, core in ((send_ref, 1 - place.core), (keep_ref, place.core)):
        total = 0.0
        for hidden_ref, grad in zip(hidden_refs, grads):
            total = total + across(hidden_ref[:, at(core, share)], grad)
        out_ref[...] = total.astype(bf16)
        give(0 if out_ref is keep_ref else 1)


def cast_near_kernel(here, scalars, take, made, give, scratch):
    place = here(scalars[0])
    up_ref, down_ref = made
    up_ref[...] = take(0)[:, at(place.chip, up_ref.shape[1])].astype(bf16)
    give(0)
    down_ref[...] = take(1)[...].astype(bf16)


def taps_kernel(here, scalars, take, made, give, scratch):
    grad_ref, head_ref, tail_ref, terms_ref = made
    pad_ref, shift_ref = scratch
    place = here(scalars[0])
    length, width = grad_ref.shape
    side = head_ref.shape[0]
    spots, back_ref = take(0)[...], take(5)
    slots = spots.shape[0]
    features = 0.0
    for chip in range(back_ref.shape[0] // slots):
        features = features + across(spots, back_ref[chip * slots : (chip + 1) * slots, :])
    features = features.astype(bf16).astype(f32)
    grad = (features * take(1)[...].astype(f32)).astype(bf16)
    grad_ref[...] = grad
    head_ref[...] = grad[:side]
    tail_ref[...] = grad[length - side :]
    give(1)
    give(2)
    give(0)
    left, frames, right = take(2), take(3), take(4)
    shift_ref[0:8, :] = jnp.zeros((8, 128), f32)
    shift_ref[8 + length :, :] = jnp.zeros((8, 128), f32)
    strips = width // 128
    for step in range(strips):
        cols = slice(step * 128, (step + 1) * 128)
        fill_padded(pad_ref, place, left, frames, right, cols)
        shift_ref[8 : 8 + length, :] = grad_ref[:, cols].astype(f32)
        for rest in range(8):
            moved = shift_ref[8 - rest : 8 - rest + length + 8, :]
            for tap in range(rest, terms_ref.shape[0] // strips * 8, 8):
                product = moved * pad_ref[tap - rest : tap - rest + length + 8, :]
                tile = tap // 8 * strips + step
                terms_ref[tile, rest : rest + 1, :] = jnp.sum(product, axis=0, keepdims=True)


def frames_kernel(here, scalars, take, made, give, scratch):
    (out_ref,) = made
    pad_ref, shift_ref = scratch
    place = here(scalars[0])
    length, width = out_ref.shape
    left, grad, right, taps_ref, cot_ref = take(0), take(1), take(2), take(3), take(4)
    count = taps_ref.shape[0]

    def lanes(step, carry):
        cols = at(step, 128)
        fill_padded(pad_ref, place, left, grad, right, cols)
        weights = [None] + [taps_ref[tap : tap + 1, cols] for tap in range(count - 1, -1, -1)]
        total = slide(pad_ref, shift_ref, weights, length)
        out_ref[:, cols] = (cot_ref[:, cols].astype(f32) + total).astype(bf16)
        return carry

    lax.fori_loop(0, width // 128, lanes, 0)


def spread_kernel(scalars, take, made, give, scratch):
    total = jnp.sum(take(0)[...], axis=0, keepdims=True)
    made[0][...] = jnp.broadcast_to(total, made[0].shape)


def adam_kernel(
    here, sums, index_ref, master_ref, mean_ref, mean_scale_ref, square_ref, square_scale_ref, *refs
):
    keep_ref, theirs_ref, far_refs, refs = refs[0], refs[1], refs[2 : 2 + sums], refs[2 + sums :]
    next_ref, mean_next_ref, mean_top_ref, square_next_ref, square_top_ref = refs[:5]
    split_ref, spread_ref, tops_ref, grad_ref = refs[5:]
    rows, width = master_ref.shape
    blocks = mean_scale_ref.shape[0]
    size = width // blocks
    units = keep_ref.shape[1]
    step = pl.program_id(0)
    steps = pl.num_programs(0)

    @pl.when(step == 0)
    def _():
        lane = lax.broadcasted_iota(jnp.int32, (128, width), 0)
        entry = lax.broadcasted_iota(jnp.int32, (128, width), 1)
        chosen = (lax.rem(lane, blocks) == entry // size) & (lane < 3 * blocks)
        spread_ref[...] = chosen.astype(f32).astype(bf16)
        split_ref[...] = jnp.zeros_like(split_ref)
        for kind, scale_ref in enumerate((mean_scale_ref, square_scale_ref)):
            rest = scale_ref[...]
            for term in range(3):
                piece = rest.astype(bf16).astype(f32)
                split_ref[kind, :, term * blocks : (term + 1) * blocks] = piece.T
                rest = rest - piece

    place = here(index_ref)
    near = slice(0, width) if units == width else at(place.chip, units)
    grad_ref[:, near] = keep_ref[...].astype(f32) + theirs_ref[...].astype(f32)
    for index, far_ref in enumerate(far_refs):
        grad_ref[:, at(place.came[index + 1], units)] = far_ref[...].astype(f32)

    part = at(step, rows)
    mean_scales, square_scales = [
        jnp.dot(
            split_ref[kind, part, :].astype(bf16), spread_ref[...], preferred_element_type=f32
        )
        for kind in range(2)
    ]
    for block in range(blocks):
        cols = slice(block * size, (block + 1) * size)
        grad = grad_ref[:, cols]
        mean = beta_one * (
            mean_ref[:, cols].astype(f32) * mean_scales[:, cols]
        ) + (1.0 - beta_one) * grad
        square = beta_two * (
            square_ref[:, cols].astype(f32) * square_scales[:, cols]
        ) + (1.0 - beta_two) * (grad * grad)
        root = jnp.sqrt(square * (1.0 / bias_two)) + adam_eps
        next_ref[:, cols] = master_ref[:, cols] - (learn_rate / bias_one) * (mean / root)
        mean_top = jnp.max(jnp.abs(mean), axis=1, keepdims=True) + scale_eps
        square_top = jnp.max(square, axis=1, keepdims=True) + scale_eps
        mean_next_ref[:, cols] = (mean * (1.0 / mean_top)).astype(bf16)
        square_next_ref[:, cols] = (square * (1.0 / square_top)).astype(bf16)
        tops_ref[0, part, block : block + 1] = mean_top
        tops_ref[1, part, block : block + 1] = square_top

    @pl.when(step == steps - 1)
    def _():
        mean_top_ref[...] = tops_ref[0, :, :blocks].T
        square_top_ref[...] = tops_ref[1, :, :blocks].T


def adam(name, here, index, master, grads, mean_code, mean_scale, square_code, square_scale):
    _, rows, width = master.shape
    blocks = mean_scale.shape[-1]
    part = min(rows, (1 << 18) // width)
    tile = pl.BlockSpec((part, width), lambda i: (i, 0))
    whole = pl.BlockSpec((blocks, rows), lambda i: (0, 0))
    pieces = [pl.BlockSpec((part, grad.shape[1]), lambda i: (i, 0)) for grad in grads]
    wide = jax.ShapeDtypeStruct((rows, width), f32)
    code = jax.ShapeDtypeStruct((rows, width), bf16)
    scale = jax.ShapeDtypeStruct((blocks, rows), f32)
    results = pl.pallas_call(
        functools.partial(adam_kernel, here, len(grads) - 2),
        grid=(rows // part,),
        out_shape=[wide, code, scale, code, scale],
        in_specs=[pl.BlockSpec(memory_space=pltpu.SMEM), tile, tile, whole, tile, whole] + pieces,
        out_specs=[tile, tile, whole, tile, whole],
        scratch_shapes=[
            pltpu.VMEM((2, rows, 128), f32),
            pltpu.VMEM((128, width), bf16),
            pltpu.VMEM((2, rows, 128), f32),
            pltpu.VMEM((part, width), f32),
        ],
        compiler_params=pltpu.CompilerParams(vmem_limit_bytes=VMEM_BYTES),
        cost_estimate=pl.CostEstimate(
            flops=20 * rows * width,
            bytes_accessed=(16 + 2 * len(grads)) * rows * width,
            transcendentals=0,
        ),
        name=name,
    )(index, master[0], mean_code[0], mean_scale[0].T, square_code[0], square_scale[0].T, *grads)
    new_master, mean_next, mean_top, square_next, square_top = results
    return (new_master[None], mean_next[None], mean_top.T[None], square_next[None], square_top.T[None])


def by_expert(rows):
    experts = lax.axis_size("expert")
    slots, width = rows.shape
    cells = rows.reshape(experts, slots // experts, width)
    return lax.all_to_all(cells, "expert", 0, 0, tiled=True).reshape(slots, width)


def to_senders(rows):
    axes = ("chip", "expert")
    count = lax.axis_size("chip") * lax.axis_size("expert")
    cells = rows.reshape(count, rows.shape[0] // count, rows.shape[1])
    return lax.all_to_all(cells, axes, 0, 0, tiled=True).reshape(rows.shape)


def to_chip(values, shift):
    chips = lax.axis_size("chip")
    return lax.ppermute(values, "chip", [(i, (i + shift) % chips) for i in range(chips)])


def to_core(values):
    return lax.ppermute(values, "core", [(0, 1), (1, 0)])


def halo(head, tail):
    axes = ("chip", "core", "expert")
    count = math.prod(lax.axis_size(axis) for axis in axes)
    right = [(i, (i + 1) % count) for i in range(count)]
    left = [((i + 1) % count, i) for i in range(count)]
    return lax.ppermute(tail, axes, right), lax.ppermute(head, axes, left)


def sum_everywhere(terms, strips, after):
    axes = ("chip", "core", "expert")
    count = math.prod(lax.axis_size(axis) for axis in axes)
    tiles, rows, lanes = terms.shape
    cells = terms.reshape(count, tiles * rows // count, lanes)
    parts = lax.all_to_all(cells, axes, 0, 0, tiled=True)
    (spread,) = call(spread_kernel, "spread", [], [parts], [(cells.shape, f32)], after=after)
    total = lax.all_to_all(spread, axes, 0, 0, tiled=True)
    total = total.reshape(tiles // strips, strips, rows, lanes).transpose(0, 2, 1, 3)
    return total.reshape(tiles // strips * rows, strips * lanes)


def body(
    frames,
    cotangent,
    expert_ids,
    conv_weight,
    up_master,
    down_master,
    up_mean_code,
    up_mean_scale,
    up_square_code,
    up_square_scale,
    down_mean_code,
    down_mean_scale,
    down_square_code,
    down_square_scale,
):
    length, width = frames.shape
    taps = conv_weight.shape[0]
    side = taps // 2
    experts = lax.axis_size("expert")
    chips = lax.axis_size("chip")
    dp_size = 2 * chips
    capacity = 2 * length // experts
    slots = experts * capacity
    hidden = up_master.shape[2]
    index = lax.axis_index(("chip", "core", "expert"))
    index = index.astype(jnp.int32).reshape(1)
    here = functools.partial(Place, dp_size, experts)
    product = 2 * slots * width * hidden // chips
    row_shape = ((slots, width), bf16)
    strips = [pltpu.VMEM((length + 2 * side + 8, 128), f32), pltpu.VMEM((length + 16, 128), f32)]
    share, depth, units = hidden // dp_size, width // dp_size, hidden // chips

    head, tail, place, send_grads, *up_parts = call(
        functools.partial(prepare_kernel, here, experts, capacity),
        "prepare",
        [index],
        [expert_ids.reshape(1, length), cotangent, frames, up_master[0]],
        [((side, width), bf16)] * 2
        + [((slots, length), bf16), row_shape]
        + [((depth, units), bf16)] * (chips - 1),
        flops=2 * slots * length * width,
        moved=4 * slots * width,
    )
    left, right = halo(head, tail)
    far_ups = [to_chip(part, shift + 1) for shift, part in enumerate(up_parts)]
    up_own, down_own = call(
        functools.partial(cast_near_kernel, here),
        "cast_near",
        [index],
        [up_master[0], down_master[0]],
        [((depth, units), bf16), ((share, width), bf16)],
        after=[place],
        moved=12 * share * width,
    )
    ups = [up_own, to_core(up_own)]
    downs = [down_own, to_core(down_own)]
    for arrived in far_ups:
        ups = ups + [arrived, to_core(arrived)]
    grads_in = by_expert(send_grads)
    (inner,) = call(
        conv_kernel,
        "convolve",
        [],
        [frames, conv_weight],
        [((length, width), f32)],
        scratch=strips,
        after=[down_own],
        flops=2 * slots * length * width,
        moved=8 * slots * width,
    )
    slope, send_rows = call(
        functools.partial(edge_kernel, here),
        "edges",
        [index],
        [left, right, inner, conv_weight, place],
        [((length, width), bf16), row_shape],
        after=far_ups + [down_own],
        scratch=strips + [pltpu.VMEM((length, width), bf16)],
        flops=2 * slots * length * width,
        moved=8 * slots * width,
    )
    rows_in = by_expert(send_rows)

    spans = [(rows_in, grads_in)]
    for shift in range(1, chips):
        spans.append((to_chip(rows_in, shift), to_chip(grads_in, shift)))
    hiddens, pres, parts = [], [], []
    for turn, (rows, grads) in enumerate(spans):
        last = turn == chips - 1
        results = call(
            functools.partial(group_kernel, here, turn if last else 0),
            "far_group" if turn else "own_group",
            [index],
            [rows] + ups + [grads] + downs + (parts if last else []),
            [
                ((slots, units), bf16),
                ((slots, units), bf16),
                ((chips * slots if last else slots, width), bf16),
            ],
            scratch=[pltpu.VMEM((slots, units), f32)],
            after=parts[-1:],
            flops=3 * product,
            moved=8 * width * units,
        )
        for kind, result in zip((hiddens, pres, parts), results):
            kind.append(result)
    returned = to_senders(parts[-1])
    group_rows = [rows for rows, _ in spans]
    group_grads = [grads for _, grads in spans]
    up_keep, up_send = call(
        functools.partial(up_grad_kernel, here, len(spans)),
        "up_grad",
        [index],
        group_rows + pres,
        [((chips * depth, units), bf16)] * 2,
        flops=chips * product,
        moved=8 * width * units,
    )
    up_theirs = to_core(up_send)
    up_grads = [up_keep, up_theirs]
    for shift in range(1, chips):
        part = slice(shift * depth, (shift + 1) * depth)
        chip_sum = (up_keep[part].astype(f32) + up_theirs[part].astype(f32)).astype(bf16)
        up_grads.append(to_chip(chip_sum, shift))
    down_keep, down_send = call(
        functools.partial(down_grad_kernel, here, len(spans)),
        "down_grad",
        [index],
        hiddens + group_grads,
        [((share, width), bf16)] * 2,
        flops=chips * product,
        moved=8 * width * units,
    )
    down_grads = [down_keep, to_core(down_send)]

    down_next = adam(
        "adam_down", here, index, down_master, down_grads,
        down_mean_code, down_mean_scale, down_square_code, down_square_scale,
    )
    grad_conv, head, tail, conv_terms = call(
        functools.partial(taps_kernel, here),
        "taps",
        [index],
        [place, slope, left, frames, right, returned],
        [((length, width), bf16), ((side, width), bf16), ((side, width), bf16), ((taps // 8 * (width // 128), 8, 128), f32)],
        after=[down_next[0]],
        scratch=strips,
        flops=2 * slots * length * width,
        moved=8 * slots * width,
    )
    grad_left, grad_right = halo(head, tail)
    (grad_frames,) = call(
        functools.partial(frames_kernel, here),
        "frames",
        [index],
        [grad_left, grad_conv, grad_right, conv_weight, cotangent],
        [((length, width), bf16)],
        scratch=strips,
        flops=2 * slots * length * width,
        moved=4 * slots * width,
    )
    up_next = adam(
        "adam_up", here, index, up_master, up_grads,
        up_mean_code, up_mean_scale, up_square_code, up_square_scale,
    )
    conv_total = sum_everywhere(conv_terms, width // 128, [up_next[0], grad_left, grad_right])
    return (grad_frames, conv_total) + up_next + down_next


def solution(mesh):
    dp_size, experts = mesh.shape["dp"], mesh.shape["expert"]
    devices = mesh.devices.reshape(dp_size // 2, 2, experts)
    finer = jax.sharding.Mesh(devices, ("chip", "core", "expert"))
    frames = P(("chip", "core", "expert"), None)
    shared = P()
    state = P("expert", ("chip", "core"), None)
    return jax.shard_map(
        body,
        mesh=finer,
        in_specs=(frames,) * 3 + (shared,) + (state,) * 10,
        out_specs=(frames, shared) + (state,) * 10,
        check_vma=False,
    )
```
